32 devices in a mesh: scen: 4 (over y, x), blk: 8 (over z, core).
Axes of the slice: x: 2, y: 2, z: 4, core: 2. Of those that a mesh axis runs over, the one named last changes fastest.
Arguments:
- link: bfloat16 [16, 256, 4096], P('scen', None, 'blk'), may hold values from -0.3125 to 0.3125
- leaf_inverse: bfloat16 [16, 256, 256], P('scen'), as said below
- leaf_rhs: float32 [16, 256], P('scen'), may hold values from -6 to 6
- node_rhs: float32 [2, 4096], P(None, 'blk'), may hold values from -6 to 6
- node_diag: float32 [2, 4096], P(None, 'blk'), may hold values from 0.5 to 4
- parent: int32 [16], P('scen'), may hold values from 0 to 1
- tile_mask: int32 [16, 8], P('scen', 'blk'), may hold values 0 or 1
Outputs:
- node_solution: float32 [2, 4096], P(None, 'blk')
- leaf_solution: float32 [16, 256], P('scen')
- schur: float32 [2, 4096, 4096], P(None, 'blk', 'scen')
The draws below stay inside these ranges and needn't reach their ends.
Inputs may be any that keep to these rules, and one draw needn't show every extreme that they name: `leaf_inverse`: its diagonal entries lie within 1 to 2.
All inputs are finite; a program needn't handle non-finite values. No bound on the sum of `tile_mask` on one device may be relied on, other than what follows from the above.
Results may differ from the reference program's by a relative error of at most 0.0017.
Values may be sent and summed in bfloat16 or wider, within the bound.
No kernel may reach another device: no remote copies, remote signals or barrier semaphores. Data moves between devices by JAX's collectives and lax.ppermute only.
A program may use at most 256 MiB of HBM per device.

```python
import math
import jax
import jax.numpy as jnp
from jax import lax

NP = 4096
NL = 256
NODES = 2
ITERS = 4
LEAVES = 16
TILES = 8


def draw_leaf_inverse(key, part):
    key_off = jax.random.fold_in(key, 11)
    key_diag = jax.random.fold_in(key, 12)
    noise_draw = jax.random.uniform(key_off, (LEAVES, NL, NL), jnp.float32, -1.0, 1.0)
    symmetric = 0.42 * (noise_draw + jnp.swapaxes(noise_draw, 1, 2)) / NL ** 0.5
    leading = jax.random.uniform(key_diag, (LEAVES, NL, 1), jnp.float32, 1.0, 2.0)
    on_diag = lax.broadcasted_iota(jnp.int32, (NL, NL), 0) == lax.broadcasted_iota(jnp.int32, (NL, NL), 1)
    return jnp.where(on_diag[None], leading, symmetric).astype(jnp.bfloat16)


def with_ends(array, rng, least, high):
    spot = [jax.random.randint(jax.random.fold_in(rng, axis), (), 0, length) for axis, length in enumerate(array.shape)]
    longest = array.shape.index(max(array.shape))
    neighbour = spot[:longest] + [(spot[longest] + 1) % array.shape[longest]] + spot[longest + 1:]
    return array.at[tuple(spot)].set(least).at[tuple(neighbour)].set(high)


def block_levels(stream_key, extent, pieces, low, largest):
    level, own = 1.0, jax.random.fold_in(stream_key, 6)
    for axis_at, shards_of in pieces:
        steps = jnp.exp(jax.random.uniform(jax.random.fold_in(own, axis_at), (shards_of,), jnp.float32, low / len(pieces), largest / len(pieces)))
        level = level * jnp.repeat(steps, extent[axis_at] // shards_of).reshape([-1 if axis == axis_at else 1 for axis in range(len(extent))])
    return level


def centred(rng, dims, width, most, shards=(), held_as=jnp.bfloat16):
    values = width * jax.random.normal(rng, dims, jnp.float32)
    if shards:
        values = values * block_levels(rng, dims, shards, -0.22, 0.18)
    return jnp.clip(values, -most, most).astype(held_as)


def setup_inputs(seed: int = 0) -> dict:
    keys = jax.random.split(jax.random.key(seed), 8)
    link = centred(keys[0], (LEAVES, NL, NP), (NL * LEAVES // NODES // 6) ** -0.5, 0.3125, ((0, 4), (2, 8)))
    leaf_inverse = draw_leaf_inverse(jax.random.fold_in(keys[7], 71), 0)
    leaf_rhs = centred(keys[2], (LEAVES, NL), 1.0, 6.0, ((0, 4),), jnp.float32)
    node_rhs = centred(keys[3], (NODES, NP), 1.0, 6.0, ((1, 8),), jnp.float32)
    node_diag = jnp.clip(jnp.exp(math.log(4.0) - 2.0794415 * jax.random.uniform(keys[4], (NODES, NP), jnp.float32) ** block_levels(keys[4], (NODES, NP), ((1, 8),), -0.2, 0.2)), 0.5, 4.0)
    parent = with_ends(jax.random.randint(keys[5], (LEAVES,), 0, NODES), jax.random.fold_in(keys[5], 1), 0, NODES - 1).astype(jnp.int32)
    tile_mask = with_ends((jax.random.randint(keys[6], (LEAVES, TILES), 0, 2) < 1).astype(jnp.int32), jax.random.fold_in(keys[6], 1), 0, 1)
    return {"link": link, "leaf_inverse": leaf_inverse, "leaf_rhs": leaf_rhs, "node_rhs": node_rhs, "node_diag": node_diag, "parent": parent, "tile_mask": tile_mask}


highest = lax.Precision.HIGHEST
damping = 0.4


def reference(link, leaf_inverse, leaf_rhs, node_rhs, node_diag, parent, tile_mask):
    leaf_count, width_leaf, full_width = link.shape
    node_count = node_rhs.shape[0]
    tile_count = tile_mask.shape[1]
    tile_width = full_width // tile_count
    column_mask = jnp.repeat(tile_mask.astype(jnp.bfloat16), tile_width, axis=1)
    masked = link * column_mask[:, None, :]
    inverse_f = leaf_inverse.astype(jnp.float32)
    masked_f = masked.astype(jnp.float32)
    solved = jnp.einsum("lnm,lmc->lnc", inverse_f, masked_f, precision=highest).astype(jnp.bfloat16)

    def accumulate(carry, items):
        link_rows, solved_rows, owner = items
        update = jnp.dot(link_rows.astype(jnp.float32).T, solved_rows.astype(jnp.float32), precision=highest)
        return carry.at[owner].add(update), None

    start_blocks = jnp.zeros((node_count, full_width, full_width), jnp.float32)
    schur, unused = lax.scan(accumulate, start_blocks, (masked, solved, parent))
    ownership = (parent[:, None] == jnp.arange(node_count, dtype=jnp.int32)[None, :]).astype(jnp.float32)
    leaf_solve = jnp.einsum("lnm,lm->ln", inverse_f, leaf_rhs, precision=highest)
    leaf_terms = jnp.einsum("lnc,ln->lc", masked_f, leaf_solve, precision=highest)
    reduced = node_rhs - jnp.dot(ownership.T, leaf_terms, precision=highest)
    scaling = node_diag + jnp.diagonal(schur, axis1=1, axis2=2)
    current = reduced / scaling
    for sweep in range(ITERS):
        product = node_diag * current + jnp.einsum("prc,pc->pr", schur, current, precision=highest)
        current = current + damping * (reduced - product) / scaling
    parent_values = jnp.dot(ownership, current, precision=highest)
    coupling = jnp.einsum("lnc,lc->ln", masked_f, parent_values, precision=highest)
    leaf_solution = jnp.einsum("lnm,lm->ln", inverse_f, leaf_rhs - coupling, precision=highest)
    return current, leaf_solution, schur
```

```python
import functools

import jax
import jax.numpy as jnp
from jax import lax
from jax.experimental import pallas as pl
from jax.experimental.pallas import tpu as pltpu
from jax.sharding import PartitionSpec as P

ITERS = 4
highest = lax.Precision.HIGHEST
damping = 0.4
F32 = jnp.float32
BF16 = jnp.bfloat16
MIB = 1 << 20

VM = pl.BlockSpec(memory_space=pltpu.VMEM)
SM = pl.BlockSpec(memory_space=pltpu.SMEM)
HB = pl.BlockSpec(memory_space=pl.ANY)
NO_COST = pl.CostEstimate(flops=0, bytes_accessed=0, transcendentals=0)


def general_body(link, leaf_inverse, leaf_rhs, node_rhs, node_diag, parent, tile_mask):
    leaf_count, width_leaf, tile_width = link.shape
    node_count = node_rhs.shape[0]
    blk_index = lax.axis_index("blk")
    node_ids = lax.broadcasted_iota(jnp.int32, (leaf_count, node_count), 1)
    member = parent[:, None] == node_ids
    member_f = member.astype(F32)
    masked = link * tile_mask.astype(BF16)[:, :, None]
    solved = jnp.einsum("lnm,lmc->lnc", leaf_inverse, masked, preferred_element_type=F32).astype(BF16)
    chosen = masked[None] * member.astype(BF16).T[:, :, None, None]
    chosen = chosen.reshape(node_count, leaf_count * width_leaf, tile_width)
    portion = lax.all_gather(solved, "blk", axis=2, tiled=True)
    stacked = portion.reshape(leaf_count * width_leaf, portion.shape[2])
    partial_value = jnp.einsum("pkr,kc->prc", chosen, stacked, preferred_element_type=F32)
    diagonal_tile = lax.dynamic_slice_in_dim(partial_value, blk_index * tile_width, tile_width, 2)
    diag_terms = jnp.diagonal(diagonal_tile, axis1=1, axis2=2)
    inverse_f = leaf_inverse.astype(F32)
    masked_f = masked.astype(F32)
    leaf_solve = jnp.einsum("lnm,lm->ln", inverse_f, leaf_rhs, precision=highest)
    leaf_terms = jnp.einsum("lnc,ln->lc", masked_f, leaf_solve, precision=highest)
    rhs_terms = jnp.dot(member_f.T, leaf_terms, precision=highest)
    rhs_sum, diag_sum = lax.psum((rhs_terms, diag_terms), "scen")
    reduced = node_rhs - rhs_sum
    scaling = node_diag + diag_sum
    schur_rows = lax.psum_scatter(partial_value, "scen", scatter_dimension=1, tiled=True)
    schur_out = lax.all_to_all(schur_rows, "scen", split_axis=2, concat_axis=1, tiled=True)
    solved_f = solved.astype(F32)
    current = reduced / scaling
    for sweep in range(ITERS):
        parent_tile = jnp.dot(member_f, current, precision=highest)
        local_image = jnp.einsum("lnc,lc->ln", solved_f, parent_tile, precision=highest)
        leaf_image = lax.psum(local_image, "blk")
        spread = jnp.einsum("lnc,ln->lc", masked_f, leaf_image, precision=highest)
        node_terms = jnp.dot(member_f.T, spread, precision=highest)
        coupled = lax.psum(node_terms, "scen")
        product = node_diag * current + coupled
        current = current + damping * (reduced - product) / scaling
    parent_values = jnp.dot(member_f, current, precision=highest)
    link_term = jnp.einsum("lnc,lc->ln", masked_f, parent_values, precision=highest)
    summed = lax.psum(link_term, "blk")
    leaf_solution = jnp.einsum("lnm,lm->ln", inverse_f, leaf_rhs - summed, precision=highest)
    return (current, leaf_solution, schur_out)


def split3(x):
    hi = x.astype(BF16)
    rest = x - hi.astype(F32)
    mid = rest.astype(BF16)
    low = (rest - mid.astype(F32)).astype(BF16)
    row = lax.broadcasted_iota(jnp.int32, (8, x.shape[1]), 0)
    wide = lambda v: jnp.broadcast_to(v.astype(F32), (8, x.shape[1]))
    out = jnp.where(row == 0, wide(hi), jnp.where(row == 1, wide(mid), jnp.where(row == 2, wide(low), 0.0)))
    return out.astype(BF16)


def rowdot(x, mat, transposed):
    dims = (((1,), (1 if transposed else 0,)), ((), ()))
    return jnp.sum(lax.dot_general(split3(x), mat, dims, preferred_element_type=F32), axis=0, keepdims=True)


def start_kernel(leaves, width, core_ref, mask_ref, parent_ref, link_ref, inverse_ref, rhs_ref, bundle_ref, notes_ref):
    half = leaves // 2
    base = leaves * width
    for i in range(half):
        bundle_ref[pl.ds(base, width), pl.ds(i * width, width)] = inverse_ref[core_ref[0] * half + i]
    notes_ref[...] = jnp.zeros_like(notes_ref)
    value = rhs_ref[...]
    for n in range(3):
        term = value.astype(BF16).astype(F32)
        notes_ref[pl.ds(n * leaves, leaves), pl.ds(0, width)] = term
        value = value - term
    for l in range(leaves):
        notes_ref[pl.ds(3 * leaves + l, 1), :] = jnp.full((1, notes_ref.shape[1]), parent_ref[l].astype(F32))
    bundle_ref[pl.ds(base + width, 4 * leaves), :] = notes_ref[...].astype(BF16)
    for l in range(leaves):
        rows = pl.ds(l * width, width)
        tile = jnp.where(mask_ref[l] != 0, link_ref[l].astype(F32), 0.0).astype(BF16)
        bundle_ref[rows, :] = tile


def solved_kernel(leaves, width, bundle_ref, inverse_ref, solved_ref):
    for l in range(leaves):
        rows = pl.ds(l * width, width)
        solved_ref[rows, :] = jnp.dot(inverse_ref[l], bundle_ref[rows, :], preferred_element_type=F32).astype(BF16)


def cut_kernel(x_hbm, y_hbm, *refs):
    top_ref, end_ref, sem = refs[-3:]
    cut = top_ref.shape[0]
    copies = [pltpu.make_async_copy(x_hbm.at[pl.ds(0, cut)], top_ref, sem.at[0]),
              pltpu.make_async_copy(y_hbm.at[pl.ds(cut, end_ref.shape[0])], end_ref, sem.at[1])]
    for copy in copies:
        copy.start()
    for copy in copies:
        copy.wait()


def node_add(acc, parent, value):
    return [jnp.where(parent == p, a + value, a) for p, a in enumerate(acc)]


def tree(groups):
    while len(groups) > 1:
        groups = [[a + b for a, b in zip(groups[i], groups[i + 1])] for i in range(0, len(groups), 2)]
    return groups[0]


def image_rows(mat_ref, at, split, parent):
    lhs = split[0]
    for q in range(1, len(split)):
        lhs = jnp.where(parent == q, split[q].astype(F32), lhs.astype(F32)).astype(BF16)
    out = lax.dot_general(lhs, mat_ref[at, :], (((1,), (1,)), ((), ())), preferred_element_type=F32)
    return jnp.sum(out, axis=0, keepdims=True)


def group_work(leaves, width, first_leaf, group, tile_of, inv_of, m_ref, km_ref, rhs_ref, parent_ref, nodes, cols):
    zero = jnp.zeros((1, cols), F32)
    diag, right = [zero] * nodes, [zero] * nodes
    for i in range(leaves):
        l = first_leaf + i
        rows = pl.ds((group * leaves + i) * width, width)
        inv, tile = inv_of(i), tile_of(i)
        m_ref[rows, :] = tile
        solved = jnp.dot(inv, tile, preferred_element_type=F32).astype(BF16)
        km_ref[rows, :] = solved
        p = parent_ref[l]
        diag = node_add(diag, p, jnp.sum(tile.astype(F32) * solved.astype(F32), axis=0, keepdims=True))
        leaf = rowdot(rhs_ref[pl.ds(l, 1), :], inv, True)
        right = node_add(right, p, rowdot(leaf, tile, False))
    return diag, right


def tile_in(leaves, width, cut, top_ref, end_ref):
    def tile(i):
        top = min(max(cut - i * width, 0), width)
        parts = []
        if top:
            parts.append(top_ref[pl.ds(i * width, top), :])
        if top < width:
            parts.append(end_ref[pl.ds(i * width + top - cut, width - top), :])
        return parts[0] if len(parts) == 1 else jnp.concatenate(parts, axis=0)
    return tile


def pair_in(leaves, width, core_ref, own, other):
    first = core_ref[0] == 0
    own, other = own.astype(F32), other.astype(F32)
    pair = [jnp.where(first, own, other).astype(BF16), jnp.where(first, other, own).astype(BF16)]
    def inv(i):
        h, j = divmod(i, leaves // 2)
        return pair[h][:, j * width:(j + 1) * width]
    return inv


def early_kernel(leaves, width, nodes, core_ref, parent_ref, rhs_ref, inverse_ref, own_ref, x_ref, y_ref, swap_ref, m_ref, km_ref,
                 diag_ref, right_ref):
    base, cols = leaves * width, own_ref.shape[1]
    for k, ref in enumerate((own_ref, x_ref, y_ref)):
        if k:
            inv = pair_in(leaves, width, core_ref, ref[pl.ds(base, width), :], swap_ref[pl.ds((k - 1) * width, width), :])
        else:
            inv = lambda i: inverse_ref[i]
        tile = lambda i: ref[pl.ds(i * width, width), :]
        diag, right = group_work(leaves, width, k * leaves, k, tile, inv, m_ref, km_ref, rhs_ref, parent_ref, nodes, cols)
        for p in range(nodes):
            diag_ref[pl.ds(k * nodes + p, 1), :] = diag[p]
            right_ref[pl.ds(k * nodes + p, 1), :] = right[p]


def late_kernel(leaves, width, cut, core_ref, parent_ref, rhs_ref, node_rhs_ref, node_diag_ref, da_ref, db_ref, swap_ref, early_ref,
                diag_ref, right_ref, token_ref, m_ref, km_ref, reduced_ref, scaling_ref, x_ref, part_ref):
    del token_ref
    nodes, cols = node_rhs_ref.shape
    base = leaves * width
    inv = pair_in(leaves, width, core_ref, db_ref[pl.ds(base - cut, width), :], swap_ref[...])
    diag, right = group_work(leaves, width, 3 * leaves, 0, tile_in(leaves, width, cut, da_ref, db_ref), inv, m_ref, km_ref, rhs_ref,
                             parent_ref, nodes, cols)
    rows = lambda ref: [[ref[pl.ds(k * nodes + p, 1), :] for p in range(nodes)] for k in range(3)]
    diag, right = tree(rows(diag_ref) + [diag]), tree(rows(right_ref) + [right])
    start = []
    for p in range(nodes):
        at = pl.ds(p, 1)
        reduced = node_rhs_ref[at, :] - right[p]
        scaling = node_diag_ref[at, :] + diag[p]
        reduced_ref[at, :] = reduced
        scaling_ref[at, :] = scaling
        start.append(split3(reduced / scaling))
        x_ref[at, :] = reduced / scaling
    image(leaves, width, early_ref, km_ref, start, parent_ref, part_ref)


def image(leaves, width, early_ref, late_ref, split, parent_ref, part_ref):
    for l in range(4 * leaves):
        ref, at = (early_ref, l) if l < 3 * leaves else (late_ref, l - 3 * leaves)
        row = image_rows(ref, pl.ds(at * width, width), split, parent_ref[l])
        part_ref[pl.ds(l, 1), :] = row


def sweep_kernel(leaves, width, last, ties, parent_ref, y_ref, z_ref, reduced_ref, scaling_ref, diag_ref, x_in_ref, m_ref, km_ref, m3_ref,
                 km3_ref, *refs):
    x_ref, part_ref = refs[ties:]
    nodes = x_in_ref.shape[0]
    whole = y_ref[...] + z_ref[...]
    zero = jnp.zeros((1, x_in_ref.shape[1]), F32)
    groups = []
    for k in range(4):
        acc = [zero] * nodes
        for i in range(leaves):
            l = k * leaves + i
            mat = m_ref[pl.ds(l * width, width), :] if k < 3 else m3_ref[pl.ds(i * width, width), :]
            acc = node_add(acc, parent_ref[l], rowdot(whole[l:l + 1, :], mat, False))
        groups.append(acc)
    coupled = tree(groups)
    new = []
    for p in range(nodes):
        at = pl.ds(p, 1)
        x = x_in_ref[at, :]
        x = x + damping * (reduced_ref[at, :] - diag_ref[at, :] * x - coupled[p]) / scaling_ref[at, :]
        x_ref[at, :] = x
        new.append(split3(x))
    if last:
        for l in range(leaves):
            row = image_rows(m_ref, pl.ds(l * width, width), new, parent_ref[l])
            part_ref[pl.ds(l, 1), :] = row
    else:
        image(leaves, width, km_ref, km3_ref, new, parent_ref, part_ref)


def leaf_kernel(leaves, y_ref, z_ref, rhs_ref, inverse_ref, *refs):
    out_ref = refs[-1]
    rest = rhs_ref[...] - (y_ref[...] + z_ref[...])
    for l in range(leaves):
        out_ref[pl.ds(l, 1), :] = rowdot(rest[l:l + 1, :], inverse_ref[l], True)


def pick(places, sources, ties):
    shape = jax.ShapeDtypeStruct(sources[0].shape, sources[0].dtype)
    count = places.shape[0]

    def kernel(place_ref, *refs):
        first = len(sources) + len(ties)
        ins, outs, token_ref = refs[:len(sources)], refs[first:first + count], refs[first + count]
        held, sem_in, sem_out = refs[first + count + 1:]
        token_ref[...] = jnp.zeros_like(token_ref)
        for n in range(count):
            for i, source in enumerate(ins):
                @pl.when(place_ref[n] == i)
                def _():
                    pltpu.make_async_copy(source, held.at[n], sem_in.at[n]).start()
        for n in range(count):
            @pl.when(place_ref[n] >= 0)
            def _():
                pltpu.make_async_copy(ins[0], held.at[n], sem_in.at[n]).wait()
                pltpu.make_async_copy(held.at[n], outs[n], sem_out.at[n]).start()
        for n in range(count):
            @pl.when(place_ref[n] >= 0)
            def _():
                pltpu.make_async_copy(held.at[n], outs[n], sem_out.at[n]).wait()

    return pl.pallas_call(
        kernel,
        out_shape=[shape] * count + [jax.ShapeDtypeStruct((8, 128), F32)],
        in_specs=[SM] + [HB] * (len(sources) + len(ties)),
        out_specs=[HB] * count + [VM],
        scratch_shapes=[pltpu.VMEM((count,) + shape.shape, shape.dtype), pltpu.SemaphoreType.DMA((count,)),
                        pltpu.SemaphoreType.DMA((count,))],
        compiler_params=pltpu.CompilerParams(vmem_limit_bytes=56 * MIB),
        cost_estimate=NO_COST,
    )(places, *sources, *ties)


def product_kernel(leaves, width, info_ref, parent_ref, m_hbm, m3_hbm, *refs):
    near, far = refs[:8], refs[8:16]
    out_hbm, m_ref, u_ref, acc_ref, sem, out_sem = refs[16:]
    cols = m_ref.shape[1]
    base = leaves * width
    core, is_far = info_ref[0], info_ref[1]
    m_copies = [pltpu.make_async_copy(m_hbm, m_ref.at[pl.ds(0, 3 * base)], sem.at[8]),
                pltpu.make_async_copy(m3_hbm, m_ref.at[pl.ds(3 * base, base)], sem.at[9])]
    for copy in m_copies:
        copy.start()
    for n in range(8):
        for flag, group in ((0, near), (1, far)):
            @pl.when(is_far == flag)
            def _():
                pltpu.make_async_copy(group[n], u_ref.at[n], sem.at[n]).start()
    acc_ref[...] = jnp.zeros_like(acc_ref)
    for copy in m_copies:
        copy.wait()
    for side in range(2):
        for k in range(4):
            n = side * 4 + k
            pltpu.make_async_copy(near[n], u_ref.at[n], sem.at[n]).wait()

            @pl.loop(0, leaves)
            def _(i):
                tile = m_ref[pl.ds((k * leaves + i) * width, width), :]
                unit = u_ref[n, pl.ds(i * width, width), :]
                value = lax.dot_general(tile, unit, (((0,), (0,)), ((), ())), preferred_element_type=F32)
                acc_ref[side, parent_ref[k * leaves + i]] += value

        where = core if side == 0 else 1 - core
        for half in range(2):
            @pl.when(where == half)
            def _():
                pltpu.make_async_copy(acc_ref.at[side], out_hbm.at[:, :, pl.ds(half * cols, cols)], out_sem.at[side]).start()
    for side in range(2):
        pltpu.make_async_copy(acc_ref.at[side], out_hbm.at[:, :, pl.ds(0, cols)], out_sem.at[side]).wait()


def plane_body(scen, blk, link, leaf_inverse, leaf_rhs, node_rhs, node_diag, parent, tile_mask):
    leaves, width, cols = link.shape
    nodes = node_rhs.shape[0]
    base = leaves * width
    planes = blk // 2
    s, b = lax.axis_index("scen"), lax.axis_index("blk")
    z, core = b // 2, b % 2
    core1 = core.reshape(1)

    def over_scen(x, k):
        return lax.ppermute(x, "scen", [(i, i ^ k) for i in range(scen)])

    def over_z(x, step, sources):
        return lax.ppermute(x, "blk", [(2 * i + c, 2 * (i + step) + c) for i in sources for c in range(2)])

    def flip_z(x, k):
        return lax.ppermute(x, "blk", [(i, i ^ (2 * k)) for i in range(blk)])

    def flip_core(x):
        return lax.ppermute(x, "blk", [(i, i ^ 1) for i in range(blk)])

    def distance(i, j):
        return abs(i - j)

    def in_plane(x, k, far):
        pairs = [((i ^ k) * blk + 2 * j + c, i * blk + 2 * j + c) for i in range(scen) for j in range(planes) for c in range(2)
                 if (distance(i, j) == planes - 1) == far]
        return lax.ppermute(x, ("scen", "blk"), pairs)

    def flip_far(x):
        pairs = [(i * blk + 2 * j + c, i * blk + 2 * j + 1 - c) for i in range(scen) for j in range(planes) for c in range(2)
                 if distance(i, j) == planes - 1]
        return lax.ppermute(x, ("scen", "blk"), pairs)

    masks = tile_mask.reshape(leaves)
    total = base + width + 4 * leaves
    cut = base // 2 + width // 2
    call = functools.partial(pl.pallas_call, cost_estimate=NO_COST)
    struct = jax.ShapeDtypeStruct
    bundle = call(
        functools.partial(start_kernel, leaves, width),
        out_shape=struct((total, cols), BF16),
        in_specs=[SM, SM, SM, VM, VM, VM],
        out_specs=VM,
        scratch_shapes=[pltpu.VMEM((4 * leaves, cols), F32)],
    )(core1, masks, parent, link, leaf_inverse, leaf_rhs)

    bx, by = over_scen(bundle, 1), over_scen(bundle, 2)
    solved = call(
        functools.partial(solved_kernel, leaves, width),
        out_shape=struct((base, cols), BF16),
        in_specs=[VM, VM],
        out_specs=VM,
    )(bundle, leaf_inverse)
    up = {1: over_z(solved, 1, range(planes - 1))}
    down = {1: over_z(solved, -1, range(1, planes))}
    top, end = call(
        cut_kernel,
        out_shape=[struct((cut, cols), BF16), struct((total - cut, cols), BF16)],
        in_specs=[HB] * 4,
        out_specs=[VM, VM],
        scratch_shapes=[pltpu.SemaphoreType.DMA((2,))],
    )(bx, by, up[1], down[1])
    da, db = over_scen(top, 2), over_scen(end, 1)
    for step in range(2, planes - 1):
        up[step] = over_z(up[step - 1], 1, range(step - 1, planes - 1))
        down[step] = over_z(down[step - 1], -1, range(1, planes - step + 1))
    sources = [solved] + [up[i] for i in range(1, planes - 1)] + [down[i] for i in range(1, planes - 1)]

    tops = [bx[base:], by[base:], db[base - cut:]]
    swap = flip_core(jnp.concatenate([t[:width] for t in tops[:2]], axis=0))
    swap3 = flip_core(tops[2][:width])
    notes = [t[width:, :width].astype(F32) for t in tops]
    owners = [parent] + [n[3 * leaves:, 0].astype(jnp.int32) for n in notes]
    parents = jnp.concatenate(owners)
    sides = [leaf_rhs] + [n[:leaves] + n[leaves:2 * leaves] + n[2 * leaves:3 * leaves] for n in notes]
    rights, rights3 = jnp.concatenate(sides[:3], axis=0), jnp.concatenate(sides, axis=0)

    count = scen * leaves
    node_shape = struct((nodes, cols), F32)
    part_shape = struct((count, width), F32)
    early_shape, late_shape = struct((3 * base, cols), BF16), struct((base, cols), BF16)
    m_all, km_all, diag, right = call(
        functools.partial(early_kernel, leaves, width, nodes),
        out_shape=[early_shape, early_shape, struct((3 * nodes, cols), F32), struct((3 * nodes, cols), F32)],
        in_specs=[SM, SM] + [VM] * 6,
        out_specs=[VM] * 4,
        compiler_params=pltpu.CompilerParams(vmem_limit_bytes=56 * MIB),
    )(core1, jnp.concatenate(owners[:3]), rights, leaf_inverse, bundle, bx, by, swap)
    def place(column):
        away = z - column
        near = jnp.where(away >= 0, away, planes - 2 - away)
        return jnp.where(jnp.abs(away) == planes - 1, -1, near)

    edge = jnp.where(z == 1, 2 * (planes - 2), planes - 2)
    own_line, send1, send2, send3, onward, picked = pick(
        jnp.stack([place(s), place(s ^ 1), place(s ^ 2), place(s ^ 3), edge]).astype(jnp.int32), sources, [da, db, km_all])
    far0 = lax.ppermute(onward, "blk", [(2 * i + c, 2 * j + c) for i, j in ((1, 0), (planes - 2, planes - 1)) for c in range(2)])
    near = [own_line] + [in_plane(x, k + 1, False) for k, x in enumerate((send1, send2, send3))]
    far = [far0] + [in_plane(far0, k, True) for k in (1, 2, 3)]
    near_other = [flip_core(x) for x in near]
    far_other = [flip_far(x) for x in far]

    m3, km3, reduced, scaling, current, part = call(
        functools.partial(late_kernel, leaves, width, cut),
        out_shape=[late_shape, late_shape, node_shape, node_shape, node_shape, part_shape],
        in_specs=[SM, SM] + [VM] * 10,
        out_specs=[VM] * 6,
        compiler_params=pltpu.CompilerParams(vmem_limit_bytes=56 * MIB),
    )(core1, parents, rights3, node_rhs, node_diag, da, db, swap3, km_all, diag, right, picked)

    def exchange(x):
        x = x + flip_core(x)
        for step in range(planes.bit_length() - 2):
            x = x + flip_z(x, 1 << step)
        return x, flip_z(x, planes // 2)

    ties = [[far0, near[1]], near[2:3], near[3:] + near_other[:2], far[1:3] + near_other[2:3], far[3:] + near_other[3:]]
    for sweep in range(ITERS):
        last = sweep == ITERS - 1
        current, part = call(
            functools.partial(sweep_kernel, leaves, width, last, len(ties[sweep])),
            out_shape=[node_shape, struct((leaves, width), F32) if last else part_shape],
            in_specs=[SM] + [VM] * 10 + [HB] * len(ties[sweep]),
            out_specs=[VM] * 2,
            compiler_params=pltpu.CompilerParams(vmem_limit_bytes=24 * MIB),
        )(parents, *exchange(part), reduced, scaling, node_diag, current, m_all, km_all, m3, km3, *ties[sweep])
    leaf_solution = call(
        functools.partial(leaf_kernel, leaves),
        out_shape=struct((leaves, width), F32),
        in_specs=[VM] * 4 + [HB] * len(ties[ITERS]),
        out_specs=VM,
    )(*exchange(part), leaf_rhs, leaf_inverse, *ties[ITERS])

    schur = pl.pallas_call(
        functools.partial(product_kernel, leaves, width),
        out_shape=jax.ShapeDtypeStruct((nodes, cols, 2 * cols), F32),
        in_specs=[SM, SM] + [HB] * 18,
        out_specs=HB,
        scratch_shapes=[
            pltpu.VMEM((scen * base, cols), BF16),
            pltpu.VMEM((8, base, cols), BF16),
            pltpu.VMEM((2, nodes, cols, cols), F32),
            pltpu.SemaphoreType.DMA((10,)),
            pltpu.SemaphoreType.DMA((2,)),
        ],
        compiler_params=pltpu.CompilerParams(vmem_limit_bytes=56 * MIB),
        cost_estimate=NO_COST,
    )(jnp.stack([core, (jnp.abs(z - s) == planes - 1).astype(core.dtype)]).astype(jnp.int32), parents, m_all, m3,
      *near, *near_other, *far, *far_other)
    return current, leaf_solution, schur


def solution(mesh):
    scen, blk = mesh.shape["scen"], mesh.shape["blk"]
    in_specs = (
        P("scen", None, "blk"),
        P("scen", None, None),
        P("scen", None),
        P(None, "blk"),
        P(None, "blk"),
        P("scen"),
        P("scen", "blk"),
    )
    out_specs = (P(None, "blk"), P("scen", None), P(None, "blk", "scen"))
    body = functools.partial(plane_body, scen, blk) if scen == 4 and blk == 2 * scen else general_body
    return jax.shard_map(body, mesh=mesh, in_specs=in_specs, out_specs=out_specs, check_vma=False)
```

```python
import functools

import jax
import jax.numpy as jnp
from jax import lax
from jax.experimental import pallas as pl
from jax.experimental.pallas import tpu as pltpu
from jax.sharding import PartitionSpec as P

ITERS = 4
highest = lax.Precision.HIGHEST
damping = 0.4
F32 = jnp.float32
BF16 = jnp.bfloat16
MIB = 1 << 20

VM = pl.BlockSpec(memory_space=pltpu.VMEM)
SM = pl.BlockSpec(memory_space=pltpu.SMEM)
HB = pl.BlockSpec(memory_space=pltpu.HBM)
NO_COST = pl.CostEstimate(flops=0, bytes_accessed=0, transcendentals=0)


def general_body(link, leaf_inverse, leaf_rhs, node_rhs, node_diag, parent, tile_mask):
    leaf_count, width_leaf, tile_width = link.shape
    node_count = node_rhs.shape[0]
    blk_index = lax.axis_index("blk")
    node_ids = lax.broadcasted_iota(jnp.int32, (leaf_count, node_count), 1)
    member = parent[:, None] == node_ids
    member_f = member.astype(F32)
    masked = link * tile_mask.astype(BF16)[:, :, None]
    solved = jnp.einsum("lnm,lmc->lnc", leaf_inverse, masked, preferred_element_type=F32).astype(BF16)
    chosen = masked[None] * member.astype(BF16).T[:, :, None, None]
    chosen = chosen.reshape(node_count, leaf_count * width_leaf, tile_width)
    portion = lax.all_gather(solved, "blk", axis=2, tiled=True)
    stacked = portion.reshape(leaf_count * width_leaf, portion.shape[2])
    partial_value = jnp.einsum("pkr,kc->prc", chosen, stacked, preferred_element_type=F32)
    diagonal_tile = lax.dynamic_slice_in_dim(partial_value, blk_index * tile_width, tile_width, 2)
    diag_terms = jnp.diagonal(diagonal_tile, axis1=1, axis2=2)
    inverse_f = leaf_inverse.astype(F32)
    masked_f = masked.astype(F32)
    leaf_solve = jnp.einsum("lnm,lm->ln", inverse_f, leaf_rhs, precision=highest)
    leaf_terms = jnp.einsum("lnc,ln->lc", masked_f, leaf_solve, precision=highest)
    rhs_terms = jnp.dot(member_f.T, leaf_terms, precision=highest)
    rhs_sum, diag_sum = lax.psum((rhs_terms, diag_terms), "scen")
    reduced = node_rhs - rhs_sum
    scaling = node_diag + diag_sum
    schur_rows = lax.psum_scatter(partial_value, "scen", scatter_dimension=1, tiled=True)
    schur_out = lax.all_to_all(schur_rows, "scen", split_axis=2, concat_axis=1, tiled=True)
    solved_f = solved.astype(F32)
    current = reduced / scaling
    for sweep in range(ITERS):
        parent_tile = jnp.dot(member_f, current, precision=highest)
        local_image = jnp.einsum("lnc,lc->ln", solved_f, parent_tile, precision=highest)
        leaf_image = lax.psum(local_image, "blk")
        spread = jnp.einsum("lnc,ln->lc", masked_f, leaf_image, precision=highest)
        node_terms = jnp.dot(member_f.T, spread, precision=highest)
        coupled = lax.psum(node_terms, "scen")
        product = node_diag * current + coupled
        current = current + damping * (reduced - product) / scaling
    parent_values = jnp.dot(member_f, current, precision=highest)
    link_term = jnp.einsum("lnc,lc->ln", masked_f, parent_values, precision=highest)
    summed = lax.psum(link_term, "blk")
    leaf_solution = jnp.einsum("lnm,lm->ln", inverse_f, leaf_rhs - summed, precision=highest)
    return (current, leaf_solution, schur_out)


def split3(x):
    hi = x.astype(BF16)
    rest = x - hi.astype(F32)
    mid = rest.astype(BF16)
    low = (rest - mid.astype(F32)).astype(BF16)
    row = lax.broadcasted_iota(jnp.int32, (8, x.shape[1]), 0)
    wide = lambda v: jnp.broadcast_to(v.astype(F32), (8, x.shape[1]))
    out = jnp.where(row == 0, wide(hi), jnp.where(row == 1, wide(mid), jnp.where(row == 2, wide(low), 0.0)))
    return out.astype(BF16)


def rowdot(x, mat, transposed):
    dims = (((1,), (1 if transposed else 0,)), ((), ()))
    return jnp.sum(lax.dot_general(split3(x), mat, dims, preferred_element_type=F32), axis=0, keepdims=True)


def start_kernel(leaves, width, core_ref, mask_ref, parent_ref, link_ref, inverse_ref, rhs_ref, bundle_ref, notes_ref):
    half = leaves // 2
    base = leaves * width
    for i in range(half):
        bundle_ref[pl.ds(base, width), pl.ds(i * width, width)] = inverse_ref[core_ref[0] * half + i]
    notes_ref[...] = jnp.zeros_like(notes_ref)
    value = rhs_ref[...]
    for n in range(3):
        term = value.astype(BF16).astype(F32)
        notes_ref[pl.ds(n * leaves, leaves), pl.ds(0, width)] = term
        value = value - term
    for l in range(leaves):
        notes_ref[pl.ds(3 * leaves + l, 1), :] = jnp.full((1, notes_ref.shape[1]), parent_ref[l].astype(F32))
    bundle_ref[pl.ds(base + width, 4 * leaves), :] = notes_ref[...].astype(BF16)
    for l in range(leaves):
        bundle_ref[pl.ds(l * width, width), :] = masked_tile(mask_ref, link_ref, l)


def masked_tile(mask_ref, link_ref, l):
    return jnp.where(mask_ref[l] != 0, link_ref[l].astype(F32), 0.0).astype(BF16)


def solved_kernel(leaves, width, inverse_ref, bundle_ref, *refs):
    l = 0
    for ref in refs:
        for i in range(ref.shape[0] // width):
            tile = bundle_ref[pl.ds(l * width, width), :]
            ref[pl.ds(i * width, width), :] = jnp.dot(inverse_ref[l], tile, preferred_element_type=F32).astype(BF16)
            l += 1


def node_add(acc, parent, value):
    return [jnp.where(parent == p, a + value, a) for p, a in enumerate(acc)]


def tree(groups):
    while len(groups) > 1:
        groups = [[a + b for a, b in zip(groups[i], groups[i + 1])] for i in range(0, len(groups), 2)]
    return groups[0]


def image_rows(mat_ref, at, split, parent):
    lhs = split[0]
    for q in range(1, len(split)):
        lhs = jnp.where(parent == q, split[q].astype(F32), lhs.astype(F32)).astype(BF16)
    out = lax.dot_general(lhs, mat_ref[at, :], (((1,), (1,)), ((), ())), preferred_element_type=F32)
    return jnp.sum(out, axis=0, keepdims=True)


def group_work(leaves, width, first_leaf, group, tile_of, inv_of, m_ref, km_ref, rhs_ref, parent_ref, nodes, cols):
    zero = jnp.zeros((1, cols), F32)
    diag, right = [zero] * nodes, [zero] * nodes
    for i in range(leaves):
        l = first_leaf + i
        rows = pl.ds((group * leaves + i) * width, width)
        inv, tile = inv_of(i), tile_of(i)
        m_ref[rows, :] = tile
        solved = jnp.dot(inv, tile, preferred_element_type=F32).astype(BF16)
        km_ref[rows, :] = solved
        p = parent_ref[l]
        diag = node_add(diag, p, jnp.sum(tile.astype(F32) * solved.astype(F32), axis=0, keepdims=True))
        leaf = rowdot(rhs_ref[pl.ds(l, 1), :], inv, True)
        right = node_add(right, p, rowdot(leaf, tile, False))
    return diag, right


def tile_in(leaves, width, cut, top_ref, end_ref):
    def tile(i):
        top = min(max(cut - i * width, 0), width)
        parts = []
        if top:
            parts.append(top_ref[pl.ds(i * width, top), :])
        if top < width:
            parts.append(end_ref[pl.ds(i * width + top - cut, width - top), :])
        return parts[0] if len(parts) == 1 else jnp.concatenate(parts, axis=0)
    return tile


def pair_in(leaves, width, core_ref, own, other):
    first = core_ref[0] == 0
    own, other = own.astype(F32), other.astype(F32)
    pair = [jnp.where(first, own, other).astype(BF16), jnp.where(first, other, own).astype(BF16)]
    def inv(i):
        h, j = divmod(i, leaves // 2)
        return pair[h][:, j * width:(j + 1) * width]
    return inv


def early_kernel(leaves, width, nodes, core_ref, parent_ref, rhs_ref, inverse_ref, own_ref, x_ref, y_ref, swap_ref, *refs):
    m_ref, km_ref, diag_ref, right_ref = refs[-4:]
    base, cols = leaves * width, own_ref.shape[1]
    for k, ref in enumerate((own_ref, x_ref, y_ref)):
        if k:
            inv = pair_in(leaves, width, core_ref, ref[pl.ds(base, width), :], swap_ref[pl.ds((k - 1) * width, width), :])
        else:
            inv = lambda i: inverse_ref[i]
        tile = lambda i: ref[pl.ds(i * width, width), :]
        diag, right = group_work(leaves, width, k * leaves, k, tile, inv, m_ref, km_ref, rhs_ref, parent_ref, nodes, cols)
        for p in range(nodes):
            diag_ref[pl.ds(k * nodes + p, 1), :] = diag[p]
            right_ref[pl.ds(k * nodes + p, 1), :] = right[p]


def late_kernel(leaves, width, cut, core_ref, parent_ref, rhs_ref, node_rhs_ref, node_diag_ref, da_ref, db_ref, swap_ref, early_ref,
                diag_ref, right_ref, m_ref, km_ref, reduced_ref, scaling_ref, x_ref, part_ref):
    nodes, cols = node_rhs_ref.shape
    base = leaves * width
    inv = pair_in(leaves, width, core_ref, db_ref[pl.ds(base - cut, width), :], swap_ref[...])
    diag, right = group_work(leaves, width, 3 * leaves, 0, tile_in(leaves, width, cut, da_ref, db_ref), inv, m_ref, km_ref, rhs_ref,
                             parent_ref, nodes, cols)
    rows = lambda ref: [[ref[pl.ds(k * nodes + p, 1), :] for p in range(nodes)] for k in range(3)]
    diag, right = tree(rows(diag_ref) + [diag]), tree(rows(right_ref) + [right])
    start = []
    for p in range(nodes):
        at = pl.ds(p, 1)
        reduced = node_rhs_ref[at, :] - right[p]
        scaling = node_diag_ref[at, :] + diag[p]
        reduced_ref[at, :] = reduced
        scaling_ref[at, :] = scaling
        start.append(split3(reduced / scaling))
        x_ref[at, :] = reduced / scaling
    image(leaves, width, early_ref, km_ref, start, parent_ref, part_ref)


def image(leaves, width, early_ref, late_ref, split, parent_ref, part_ref):
    for l in range(4 * leaves):
        ref, at = (early_ref, l) if l < 3 * leaves else (late_ref, l - 3 * leaves)
        row = image_rows(ref, pl.ds(at * width, width), split, parent_ref[l])
        part_ref[pl.ds(l, 1), :] = row


def sweep_kernel(leaves, width, last, ties, parent_ref, y_ref, z_ref, reduced_ref, scaling_ref, diag_ref, x_in_ref, m_ref, km_ref, m3_ref,
                 km3_ref, *refs):
    x_ref, part_ref = refs[ties:]
    nodes = x_in_ref.shape[0]
    whole = y_ref[...] + z_ref[...]
    zero = jnp.zeros((1, x_in_ref.shape[1]), F32)
    groups = []
    for k in range(4):
        acc = [zero] * nodes
        for i in range(leaves):
            l = k * leaves + i
            mat = m_ref[pl.ds(l * width, width), :] if k < 3 else m3_ref[pl.ds(i * width, width), :]
            acc = node_add(acc, parent_ref[l], rowdot(whole[l:l + 1, :], mat, False))
        groups.append(acc)
    coupled = tree(groups)
    new = []
    for p in range(nodes):
        at = pl.ds(p, 1)
        x = x_in_ref[at, :]
        x = x + damping * (reduced_ref[at, :] - diag_ref[at, :] * x - coupled[p]) / scaling_ref[at, :]
        x_ref[at, :] = x
        new.append(split3(x))
    if last:
        for l in range(leaves):
            row = image_rows(m_ref, pl.ds(l * width, width), new, parent_ref[l])
            part_ref[pl.ds(l, 1), :] = row
    else:
        image(leaves, width, km_ref, km3_ref, new, parent_ref, part_ref)


def leaf_kernel(leaves, y_ref, z_ref, rhs_ref, inverse_ref, *refs):
    out_ref = refs[-1]
    rest = rhs_ref[...] - (y_ref[...] + z_ref[...])
    for l in range(leaves):
        out_ref[pl.ds(l, 1), :] = rowdot(rest[l:l + 1, :], inverse_ref[l], True)


def join(blocks, tie):
    rows = blocks[0].shape[0]

    def kernel(*refs):
        out_ref = refs[-1]
        for n in range(len(blocks)):
            out_ref[pl.ds(n * rows, rows), :] = refs[n][...]

    return pl.pallas_call(
        kernel,
        out_shape=jax.ShapeDtypeStruct((len(blocks) * rows, blocks[0].shape[1]), blocks[0].dtype),
        in_specs=[VM] * (len(blocks) + 1),
        out_specs=VM,
        compiler_params=pltpu.CompilerParams(vmem_limit_bytes=16 * MIB),
        cost_estimate=NO_COST,
    )(*blocks, tie)


def pick(places, source, ties):
    shape = jax.ShapeDtypeStruct(source.shape[1:], source.dtype)
    count = len(places)

    def kernel(place_ref, source_ref, *refs):
        first = len(ties)
        outs, token_ref = refs[first:first + count], refs[first + count]
        held, sem_in, sem_out = refs[first + count + 1:]
        token_ref[...] = jnp.zeros_like(token_ref)
        reads = [pltpu.make_async_copy(source_ref.at[place_ref[n]], held.at[n], sem_in.at[n]) for n in range(count)]
        writes = [pltpu.make_async_copy(held.at[n], outs[n], sem_out.at[n]) for n in range(count)]
        for read in reads:
            read.start()
        for read, write in zip(reads, writes):
            read.wait()
            write.start()
        for write in writes:
            write.wait()

    return pl.pallas_call(
        kernel,
        out_shape=[shape] * count + [jax.ShapeDtypeStruct((8, 128), F32)],
        in_specs=[SM, HB] + [VM] * len(ties),
        out_specs=[HB] * count + [VM],
        scratch_shapes=[pltpu.VMEM((count,) + shape.shape, shape.dtype), pltpu.SemaphoreType.DMA((count,)),
                        pltpu.SemaphoreType.DMA((count,))],
        compiler_params=pltpu.CompilerParams(vmem_limit_bytes=48 * MIB),
        cost_estimate=NO_COST,
    )(jnp.stack(places).astype(jnp.int32), source, *ties)


def product_kernel(leaves, width, parts, info_ref, parent_ref, m_hbm, m3_hbm, *refs):
    count = len(parts)
    gathered, same, other = refs[:count], refs[count:4 * count], refs[4 * count:5 * count]
    out_hbm, m_ref, u_ref, acc_ref, sem, out_sem = refs[5 * count:]
    cols = m_ref.shape[1]
    base = leaves * width
    core, column = info_ref[0], info_ref[1]
    m_copies = [pltpu.make_async_copy(m_hbm, m_ref.at[pl.ds(0, 3 * base)], sem.at[8, 0]),
                pltpu.make_async_copy(m3_hbm, m_ref.at[pl.ds(3 * base, base)], sem.at[8, 1])]
    for copy in m_copies:
        copy.start()
    loads = {}
    for side in range(2):
        place = 2 * column + (core if side == 0 else 1 - core)
        for k in range(4):
            for h in range(count):
                if k == 0:
                    source = gathered[h].at[place]
                else:
                    source = other[h].at[pl.ds((k - 1) * parts[h], parts[h])] if side else same[h * 3 + k - 1]
                n = side * 4 + k
                loads[n, h] = pltpu.make_async_copy(source, u_ref.at[n, pl.ds(sum(parts[:h]), parts[h])], sem.at[n, h])
                loads[n, h].start()
    acc_ref[...] = jnp.zeros_like(acc_ref)
    for copy in m_copies:
        copy.wait()
    for side in range(2):
        for k in range(4):
            n = side * 4 + k
            for h in range(count):
                loads[n, h].wait()

            for i in range(leaves):
                tile = m_ref[pl.ds((k * leaves + i) * width, width), :]
                unit = u_ref[n, pl.ds(i * width, width), :]
                value = lax.dot_general(tile, unit, (((0,), (0,)), ((), ())), preferred_element_type=F32)
                acc_ref[side, parent_ref[k * leaves + i]] += value

        where = core if side == 0 else 1 - core
        for half in range(2):
            @pl.when(where == half)
            def _():
                pltpu.make_async_copy(acc_ref.at[side], out_hbm.at[:, :, pl.ds(half * cols, cols)], out_sem.at[side]).start()
    for side in range(2):
        pltpu.make_async_copy(acc_ref.at[side], out_hbm.at[:, :, pl.ds(0, cols)], out_sem.at[side]).wait()


def plane_body(scen, blk, link, leaf_inverse, leaf_rhs, node_rhs, node_diag, parent, tile_mask):
    leaves, width, cols = link.shape
    nodes = node_rhs.shape[0]
    base = leaves * width
    planes = blk // 2
    s, b = lax.axis_index("scen"), lax.axis_index("blk")
    z, core = b // 2, b % 2
    core1 = core.reshape(1)

    def over_scen(x, k):
        return lax.ppermute(x, "scen", [(i, i ^ k) for i in range(scen)])

    def flip_z(x, k):
        return lax.ppermute(x, "blk", [(i, i ^ (2 * k)) for i in range(blk)])

    def flip_core(x):
        return lax.ppermute(x, "blk", [(i, i ^ 1) for i in range(blk)])

    masks = tile_mask.reshape(leaves)
    total = base + width + 4 * leaves
    cut = base // 2 + width // 2
    call = functools.partial(pl.pallas_call, cost_estimate=NO_COST, compiler_params=pltpu.CompilerParams(vmem_limit_bytes=16 * MIB))
    struct = jax.ShapeDtypeStruct
    bundle = call(
        functools.partial(start_kernel, leaves, width),
        out_shape=struct((total, cols), BF16),
        in_specs=[SM, SM, SM, VM, VM, VM],
        out_specs=VM,
        scratch_shapes=[pltpu.VMEM((4 * leaves, cols), F32)],
    )(core1, masks, parent, link, leaf_inverse, leaf_rhs)
    parts = [base - base // 4, base // 4]
    solved = call(
        functools.partial(solved_kernel, leaves, width),
        out_shape=[struct((rows, cols), BF16) for rows in parts],
        in_specs=[VM, VM],
        out_specs=[VM] * len(parts),
    )(leaf_inverse, bundle)
    gathered = [lax.all_gather(part, "blk") for part in solved]

    bx, by = over_scen(bundle, 1), over_scen(bundle, 2)
    da, db = over_scen(bx[:cut], 2), over_scen(by[cut:], 1)
    tops = [bx[base:], by[base:], db[base - cut:]]
    swap = flip_core(jnp.concatenate([t[:width] for t in tops[:2]], axis=0))
    swap3 = flip_core(tops[2][:width])
    notes = [t[width:, :width].astype(F32) for t in tops]
    owners = [parent] + [n[3 * leaves:, 0].astype(jnp.int32) for n in notes]
    parents = jnp.concatenate(owners)
    sides = [leaf_rhs] + [n[:leaves] + n[leaves:2 * leaves] + n[2 * leaves:3 * leaves] for n in notes]
    rights, rights3 = jnp.concatenate(sides[:3], axis=0), jnp.concatenate(sides, axis=0)

    count = scen * leaves
    node_shape, part_shape = pltpu.VMEM((nodes, cols), F32), pltpu.VMEM((count, width), F32)
    early_shape, late_shape = pltpu.VMEM((3 * base, cols), BF16), pltpu.VMEM((base, cols), BF16)
    terms_shape = pltpu.VMEM((3 * nodes, cols), F32)
    m_all, km_all, diag, right = call(
        functools.partial(early_kernel, leaves, width, nodes),
        out_shape=[early_shape, early_shape, terms_shape, terms_shape],
        in_specs=[SM, SM] + [VM] * 6,
        out_specs=[VM] * 4,
        compiler_params=pltpu.CompilerParams(vmem_limit_bytes=20 * MIB),
    )(core1, jnp.concatenate(owners[:3]), rights, leaf_inverse, bundle, bx, by, swap)
    def to_columns(gathered, ties):
        *blocks, token = pick([2 * (s ^ k) + core for k in (1, 2, 3)], gathered, ties)
        return [over_scen(x, k + 1) for k, x in enumerate(blocks)], token

    m3, km3, reduced, scaling, current, part = call(
        functools.partial(late_kernel, leaves, width, cut),
        out_shape=[late_shape, late_shape, node_shape, node_shape, node_shape, part_shape],
        in_specs=[SM, SM] + [VM] * 9,
        out_specs=[VM] * 6,
        compiler_params=pltpu.CompilerParams(vmem_limit_bytes=16 * MIB),
    )(core1, parents, rights3, node_rhs, node_diag, da, db, swap3, km_all, diag, right)

    def exchange(x):
        x = x + flip_core(x)
        for step in range(planes.bit_length() - 2):
            x = x + flip_z(x, 1 << step)
        return x, flip_z(x, planes // 2)

    arrived = exchange(part)
    first, token = to_columns(gathered[0], [arrived[1]])
    ties = [token]
    for sweep in range(ITERS):
        last = sweep == ITERS - 1
        current, part = call(
            functools.partial(sweep_kernel, leaves, width, last, len(ties)),
            out_shape=[struct((nodes, cols), F32), pltpu.VMEM((leaves, width), F32)] if last else [node_shape, part_shape],
            in_specs=[SM] + [VM] * 10 + [VM if tie.dtype == F32 else HB for tie in ties],
            out_specs=[VM] * 2,
            compiler_params=pltpu.CompilerParams(vmem_limit_bytes=16 * MIB),
        )(parents, *arrived, reduced, scaling, node_diag, current, m_all, km_all, m3, km3, *ties)
        arrived = exchange(part)
        ties = []
        if sweep == 1:
            ties = first
        elif sweep == 2:
            others = [flip_core(join(first, part))]
            second, token = to_columns(gathered[1], [part])
            ties = [token]
    ties = others + second
    leaf_solution = call(
        functools.partial(leaf_kernel, leaves),
        out_shape=struct((leaves, width), F32),
        in_specs=[VM] * 4 + [HB] * len(ties),
        out_specs=VM,
    )(*arrived, leaf_rhs, leaf_inverse, *ties)

    others.append(flip_core(join(second, leaf_solution)))
    schur = call(
        functools.partial(product_kernel, leaves, width, parts),
        out_shape=struct((nodes, cols, 2 * cols), F32),
        in_specs=[SM, SM] + [HB] * (2 + 5 * len(parts)),
        out_specs=HB,
        scratch_shapes=[
            pltpu.VMEM((scen * base, cols), BF16),
            pltpu.VMEM((8, base, cols), BF16),
            pltpu.VMEM((2, nodes, cols, cols), F32),
            pltpu.SemaphoreType.DMA((9, len(parts))),
            pltpu.SemaphoreType.DMA((2,)),
        ],
        compiler_params=pltpu.CompilerParams(vmem_limit_bytes=32 * MIB),
    )(jnp.stack([core, s]).astype(jnp.int32), parents, m_all, m3, *gathered, *first, *second, *others)
    return current, leaf_solution, schur


def solution(mesh):
    scen, blk = mesh.shape["scen"], mesh.shape["blk"]
    in_specs = (
        P("scen", None, "blk"),
        P("scen", None, None),
        P("scen", None),
        P(None, "blk"),
        P(None, "blk"),
        P("scen"),
        P("scen", "blk"),
    )
    out_specs = (P(None, "blk"), P("scen", None), P(None, "blk", "scen"))
    body = functools.partial(plane_body, scen, blk) if scen == 4 and blk == 2 * scen else general_body
    return jax.shard_map(body, mesh=mesh, in_specs=in_specs, out_specs=out_specs, check_vma=False)
```

```python
import functools

import jax
import jax.numpy as jnp
from jax import lax
from jax.experimental import pallas as pl
from jax.experimental.pallas import tpu as pltpu
from jax.sharding import PartitionSpec as P

ITERS = 4
highest = lax.Precision.HIGHEST
damping = 0.4
F32 = jnp.float32
BF16 = jnp.bfloat16
MIB = 1 << 20

VM = pl.BlockSpec(memory_space=pltpu.VMEM)
SM = pl.BlockSpec(memory_space=pltpu.SMEM)
HB = pl.BlockSpec(memory_space=pltpu.HBM)
NO_COST = pl.CostEstimate(flops=0, bytes_accessed=0, transcendentals=0)


def general_body(link, leaf_inverse, leaf_rhs, node_rhs, node_diag, parent, tile_mask):
    leaf_count, width_leaf, tile_width = link.shape
    node_count = node_rhs.shape[0]
    blk_index = lax.axis_index("blk")
    node_ids = lax.broadcasted_iota(jnp.int32, (leaf_count, node_count), 1)
    member = parent[:, None] == node_ids
    member_f = member.astype(F32)
    masked = link * tile_mask.astype(BF16)[:, :, None]
    solved = jnp.einsum("lnm,lmc->lnc", leaf_inverse, masked, preferred_element_type=F32).astype(BF16)
    chosen = masked[None] * member.astype(BF16).T[:, :, None, None]
    chosen = chosen.reshape(node_count, leaf_count * width_leaf, tile_width)
    portion = lax.all_gather(solved, "blk", axis=2, tiled=True)
    stacked = portion.reshape(leaf_count * width_leaf, portion.shape[2])
    partial_value = jnp.einsum("pkr,kc->prc", chosen, stacked, preferred_element_type=F32)
    diagonal_tile = lax.dynamic_slice_in_dim(partial_value, blk_index * tile_width, tile_width, 2)
    diag_terms = jnp.diagonal(diagonal_tile, axis1=1, axis2=2)
    inverse_f = leaf_inverse.astype(F32)
    masked_f = masked.astype(F32)
    leaf_solve = jnp.einsum("lnm,lm->ln", inverse_f, leaf_rhs, precision=highest)
    leaf_terms = jnp.einsum("lnc,ln->lc", masked_f, leaf_solve, precision=highest)
    rhs_terms = jnp.dot(member_f.T, leaf_terms, precision=highest)
    rhs_sum, diag_sum = lax.psum((rhs_terms, diag_terms), "scen")
    reduced = node_rhs - rhs_sum
    scaling = node_diag + diag_sum
    schur_rows = lax.psum_scatter(partial_value, "scen", scatter_dimension=1, tiled=True)
    schur_out = lax.all_to_all(schur_rows, "scen", split_axis=2, concat_axis=1, tiled=True)
    solved_f = solved.astype(F32)
    current = reduced / scaling
    for sweep in range(ITERS):
        parent_tile = jnp.dot(member_f, current, precision=highest)
        local_image = jnp.einsum("lnc,lc->ln", solved_f, parent_tile, precision=highest)
        leaf_image = lax.psum(local_image, "blk")
        spread = jnp.einsum("lnc,ln->lc", masked_f, leaf_image, precision=highest)
        node_terms = jnp.dot(member_f.T, spread, precision=highest)
        coupled = lax.psum(node_terms, "scen")
        product = node_diag * current + coupled
        current = current + damping * (reduced - product) / scaling
    parent_values = jnp.dot(member_f, current, precision=highest)
    link_term = jnp.einsum("lnc,lc->ln", masked_f, parent_values, precision=highest)
    summed = lax.psum(link_term, "blk")
    leaf_solution = jnp.einsum("lnm,lm->ln", inverse_f, leaf_rhs - summed, precision=highest)
    return (current, leaf_solution, schur_out)


def split3(x):
    hi = x.astype(BF16)
    rest = x - hi.astype(F32)
    mid = rest.astype(BF16)
    low = (rest - mid.astype(F32)).astype(BF16)
    row = lax.broadcasted_iota(jnp.int32, (8, x.shape[1]), 0)
    wide = lambda v: jnp.broadcast_to(v.astype(F32), (8, x.shape[1]))
    out = jnp.where(row == 0, wide(hi), jnp.where(row == 1, wide(mid), jnp.where(row == 2, wide(low), 0.0)))
    return out.astype(BF16)


def rowdot(x, mat, transposed):
    dims = (((1,), (1 if transposed else 0,)), ((), ()))
    return jnp.sum(lax.dot_general(split3(x), mat, dims, preferred_element_type=F32), axis=0, keepdims=True)


def start_kernel(leaves, width, core_ref, mask_ref, parent_ref, link_ref, inverse_ref, rhs_ref, bundle_ref, notes_ref):
    half = leaves // 2
    base = leaves * width
    for i in range(half):
        bundle_ref[pl.ds(base, width), pl.ds(i * width, width)] = inverse_ref[core_ref[0] * half + i]
    notes_ref[...] = jnp.zeros_like(notes_ref)
    value = rhs_ref[...]
    for n in range(3):
        term = value.astype(BF16).astype(F32)
        notes_ref[pl.ds(n * leaves, leaves), pl.ds(0, width)] = term
        value = value - term
    for l in range(leaves):
        notes_ref[pl.ds(3 * leaves + l, 1), :] = jnp.full((1, notes_ref.shape[1]), parent_ref[l].astype(F32))
    bundle_ref[pl.ds(base + width, 4 * leaves), :] = notes_ref[...].astype(BF16)
    for l in range(leaves):
        bundle_ref[pl.ds(l * width, width), :] = masked_tile(mask_ref, link_ref, l)


def masked_tile(mask_ref, link_ref, l):
    return jnp.where(mask_ref[l] != 0, link_ref[l].astype(F32), 0.0).astype(BF16)


def solved_kernel(leaves, width, inverse_ref, bundle_ref, *refs):
    for l in range(leaves):
        tile = bundle_ref[pl.ds(l * width, width), :]
        solved = jnp.dot(inverse_ref[l], tile, preferred_element_type=F32).astype(BF16)
        start = 0
        for ref in refs:
            low, high = max(l * width, start), min((l + 1) * width, start + ref.shape[0])
            if low < high:
                ref[pl.ds(low - start, high - low), :] = solved[low - l * width:high - l * width]
            start += ref.shape[0]


def node_add(acc, parent, value):
    return [jnp.where(parent == p, a + value, a) for p, a in enumerate(acc)]


def tree(groups):
    while len(groups) > 1:
        groups = [[a + b for a, b in zip(groups[i], groups[i + 1])] for i in range(0, len(groups), 2)]
    return groups[0]


def image_rows(mat_ref, at, split, parent):
    lhs = split[0]
    for q in range(1, len(split)):
        lhs = jnp.where(parent == q, split[q].astype(F32), lhs.astype(F32)).astype(BF16)
    out = lax.dot_general(lhs, mat_ref[at, :], (((1,), (1,)), ((), ())), preferred_element_type=F32)
    return jnp.sum(out, axis=0, keepdims=True)


def group_work(leaves, width, first_leaf, group, tile_of, inv_of, m_ref, km_ref, rhs_ref, parent_ref, nodes, cols):
    zero = jnp.zeros((1, cols), F32)
    diag, right = [zero] * nodes, [zero] * nodes
    for i in range(leaves):
        l = first_leaf + i
        rows = pl.ds((group * leaves + i) * width, width)
        inv, tile = inv_of(i), tile_of(i)
        m_ref[pl.ds(i * width, width), :] = tile
        solved = jnp.dot(inv, tile, preferred_element_type=F32).astype(BF16)
        km_ref[rows, :] = solved
        p = parent_ref[l]
        diag = node_add(diag, p, jnp.sum(tile.astype(F32) * solved.astype(F32), axis=0, keepdims=True))
        leaf = rowdot(rhs_ref[pl.ds(l, 1), :], inv, True)
        right = node_add(right, p, rowdot(leaf, tile, False))
    return diag, right


def tile_in(leaves, width, cut, top_ref, end_ref):
    def tile(i):
        top = min(max(cut - i * width, 0), width)
        parts = []
        if top:
            parts.append(top_ref[pl.ds(i * width, top), :])
        if top < width:
            parts.append(end_ref[pl.ds(i * width + top - cut, width - top), :])
        return parts[0] if len(parts) == 1 else jnp.concatenate(parts, axis=0)
    return tile


def pair_in(leaves, width, core_ref, own, other):
    first = core_ref[0] == 0
    own, other = own.astype(F32), other.astype(F32)
    pair = [jnp.where(first, own, other).astype(BF16), jnp.where(first, other, own).astype(BF16)]
    def inv(i):
        h, j = divmod(i, leaves // 2)
        return pair[h][:, j * width:(j + 1) * width]
    return inv


def early_kernel(leaves, width, nodes, core_ref, parent_ref, rhs_ref, inverse_ref, own_ref, x_ref, y_ref, swap_ref, *refs):
    m_refs, (km_ref, diag_ref, right_ref) = refs[:3], refs[3:]
    base, cols = leaves * width, own_ref.shape[1]
    for k, ref in enumerate((own_ref, x_ref, y_ref)):
        if k:
            inv = pair_in(leaves, width, core_ref, ref[pl.ds(base, width), :], swap_ref[pl.ds((k - 1) * width, width), :])
        else:
            inv = lambda i: inverse_ref[i]
        tile = lambda i: ref[pl.ds(i * width, width), :]
        diag, right = group_work(leaves, width, k * leaves, k, tile, inv, m_refs[k], km_ref, rhs_ref, parent_ref, nodes, cols)
        for p in range(nodes):
            diag_ref[pl.ds(k * nodes + p, 1), :] = diag[p]
            right_ref[pl.ds(k * nodes + p, 1), :] = right[p]


def late_kernel(leaves, width, cut, core_ref, parent_ref, rhs_ref, node_rhs_ref, node_diag_ref, da_ref, db_ref, swap_ref, early_ref,
                diag_ref, right_ref, m_ref, km_ref, reduced_ref, scaling_ref, x_ref, part_ref):
    nodes, cols = node_rhs_ref.shape
    base = leaves * width
    inv = pair_in(leaves, width, core_ref, db_ref[pl.ds(base - cut, width), :], swap_ref[...])
    diag, right = group_work(leaves, width, 3 * leaves, 0, tile_in(leaves, width, cut, da_ref, db_ref), inv, m_ref, km_ref, rhs_ref,
                             parent_ref, nodes, cols)
    rows = lambda ref: [[ref[pl.ds(k * nodes + p, 1), :] for p in range(nodes)] for k in range(3)]
    diag, right = tree(rows(diag_ref) + [diag]), tree(rows(right_ref) + [right])
    start = []
    for p in range(nodes):
        at = pl.ds(p, 1)
        reduced = node_rhs_ref[at, :] - right[p]
        scaling = node_diag_ref[at, :] + diag[p]
        reduced_ref[at, :] = reduced
        scaling_ref[at, :] = scaling
        start.append(split3(reduced / scaling))
        x_ref[at, :] = reduced / scaling
    image(leaves, width, early_ref, km_ref, start, parent_ref, part_ref)


def image(leaves, width, early_ref, late_ref, split, parent_ref, part_ref):
    for l in range(4 * leaves):
        ref, at = (early_ref, l) if l < 3 * leaves else (late_ref, l - 3 * leaves)
        row = image_rows(ref, pl.ds(at * width, width), split, parent_ref[l])
        part_ref[pl.ds(l, 1), :] = row


def sweep_kernel(leaves, width, last, ties, parent_ref, y_ref, z_ref, reduced_ref, scaling_ref, diag_ref, x_in_ref, m0_ref, m1_ref, m2_ref, m3_ref,
                 km_ref, km3_ref, *refs):
    m_refs = (m0_ref, m1_ref, m2_ref, m3_ref)
    x_ref, part_ref = refs[ties:]
    nodes = x_in_ref.shape[0]
    whole = y_ref[...] + z_ref[...]
    zero = jnp.zeros((1, x_in_ref.shape[1]), F32)
    groups = []
    for k in range(4):
        acc = [zero] * nodes
        for i in range(leaves):
            l = k * leaves + i
            mat = m_refs[k][pl.ds(i * width, width), :]
            acc = node_add(acc, parent_ref[l], rowdot(whole[l:l + 1, :], mat, False))
        groups.append(acc)
    coupled = tree(groups)
    new = []
    for p in range(nodes):
        at = pl.ds(p, 1)
        x = x_in_ref[at, :]
        x = x + damping * (reduced_ref[at, :] - diag_ref[at, :] * x - coupled[p]) / scaling_ref[at, :]
        x_ref[at, :] = x
        new.append(split3(x))
    if last:
        for l in range(leaves):
            row = image_rows(m0_ref, pl.ds(l * width, width), new, parent_ref[l])
            part_ref[pl.ds(l, 1), :] = row
    else:
        image(leaves, width, km_ref, km3_ref, new, parent_ref, part_ref)


def add_kernel(x_ref, y_ref, tie_ref, out_ref):
    del tie_ref
    out_ref[...] = x_ref[...] + y_ref[...]


def leaf_kernel(leaves, y_ref, z_ref, rhs_ref, inverse_ref, *refs):
    out_ref = refs[-1]
    rest = rhs_ref[...] - (y_ref[...] + z_ref[...])
    for l in range(leaves):
        out_ref[pl.ds(l, 1), :] = rowdot(rest[l:l + 1, :], inverse_ref[l], True)


def join(blocks, tie):
    rows = blocks[0].shape[0]

    def kernel(*refs):
        out_ref = refs[-1]
        for n in range(len(blocks)):
            out_ref[pl.ds(n * rows, rows), :] = refs[n][...]

    return pl.pallas_call(
        kernel,
        out_shape=jax.ShapeDtypeStruct((len(blocks) * rows, blocks[0].shape[1]), blocks[0].dtype),
        in_specs=[VM] * (len(blocks) + 1),
        out_specs=VM,
        compiler_params=pltpu.CompilerParams(vmem_limit_bytes=16 * MIB),
        cost_estimate=NO_COST,
    )(*blocks, tie)


def in_vmem(x):
    return pltpu.with_memory_space_constraint(x, pltpu.VMEM)


def in_hbm(x):
    return pltpu.with_memory_space_constraint(x, pltpu.HBM)


def pick(info, places, source, ties):
    shape = jax.ShapeDtypeStruct(source.shape[1:], source.dtype)
    count = len(places)

    def kernel(place_ref, source_ref, *refs):
        first = len(ties)
        outs, token_ref = refs[first:first + count], refs[first + count]
        held, sem_in, sem_out = refs[first + count + 1:]
        token_ref[...] = jnp.zeros_like(token_ref)
        reads = [pltpu.make_async_copy(source_ref.at[place_ref[places[n]]], held.at[n], sem_in.at[n]) for n in range(count)]
        writes = [pltpu.make_async_copy(held.at[n], outs[n], sem_out.at[n]) for n in range(count)]
        for read in reads:
            read.start()
        for read, write in zip(reads, writes):
            read.wait()
            write.start()
        for write in writes:
            write.wait()

    return pl.pallas_call(
        kernel,
        out_shape=[shape] * count + [jax.ShapeDtypeStruct((8, 128), F32)],
        in_specs=[SM, HB] + [VM] * len(ties),
        out_specs=[HB] * count + [VM],
        scratch_shapes=[pltpu.VMEM((count,) + shape.shape, shape.dtype), pltpu.SemaphoreType.DMA((count,)),
                        pltpu.SemaphoreType.DMA((count,))],
        compiler_params=pltpu.CompilerParams(vmem_limit_bytes=12 * MIB),
        cost_estimate=NO_COST,
    )(info, in_hbm(source), *ties)


def leaf_spans(width, start, rows):
    spans = []
    while rows:
        size = min(rows, width - start % width)
        spans.append((start // width, start, size))
        start, rows = start + size, rows - size
    return spans


def product_kernel(leaves, width, terms, count, fresh, side, info_ref, parent_ref, *refs):
    m_refs, sources = refs[:4], refs[4:4 + count]
    outs, (u_ref, sem, out_sem) = refs[:-3][-2 - (side is not None):], refs[-3:]
    acc_ref, token_ref = outs[:2]
    work, late, slot = [], [], 0
    for k, n, entry, offset, start, rows in terms:
        if entry is None:
            ref, offset = sources[n], offset
        else:
            copy = pltpu.make_async_copy(sources[n].at[info_ref[entry]], u_ref.at[pl.ds(slot, rows)], sem.at[len(late)])
            copy.start()
            late.append(copy)
            ref, offset = u_ref, slot
            slot += rows
        spans = [(k, leaf, at, ref, offset + at - start, size) for leaf, at, size in leaf_spans(width, start, rows)]
        work = work + spans if entry is not None else spans + work
    token_ref[...] = jnp.zeros_like(token_ref)
    if fresh:
        acc_ref[...] = jnp.zeros_like(acc_ref)
    for k, leaf, at, ref, offset, size in work:
        if ref is u_ref:
            for copy in late:
                copy.wait()
            late = []
        value = lax.dot_general(m_refs[k][pl.ds(at, size), :], ref[pl.ds(offset, size), :], (((0,), (0,)), ((), ())),
                                preferred_element_type=F32)
        acc_ref[parent_ref[k * leaves + leaf]] += value
    if side is not None:
        nodes, rows, cols = acc_ref.shape
        where = info_ref[0] if side == 0 else 1 - info_ref[0]
        size = rows // 4
        pieces = [(p, pl.ds(i * size, size)) for p in range(nodes) for i in range(4)]
        for half in range(2):
            @pl.when(where == half)
            def _():
                for n, (p, at) in enumerate(pieces):
                    pltpu.make_async_copy(acc_ref.at[p, at], outs[2].at[p, at, pl.ds(half * cols, cols)], out_sem.at[n]).start()
        for n, (p, at) in enumerate(pieces):
            pltpu.make_async_copy(acc_ref.at[p, at], outs[2].at[p, at, pl.ds(0, cols)], out_sem.at[n]).wait()


def plane_body(scen, blk, link, leaf_inverse, leaf_rhs, node_rhs, node_diag, parent, tile_mask):
    leaves, width, cols = link.shape
    nodes = node_rhs.shape[0]
    base = leaves * width
    planes = blk // 2
    s, b = lax.axis_index("scen"), lax.axis_index("blk")
    z, core = b // 2, b % 2
    info = jnp.stack([core] + [2 * (s ^ k) + c for c in (core, 1 - core) for k in range(scen)]).astype(jnp.int32)

    def over_scen(x, k):
        return lax.ppermute(x, "scen", [(i, i ^ k) for i in range(scen)])

    def flip_z(x, k):
        return lax.ppermute(x, "blk", [(i, i ^ (2 * k)) for i in range(blk)])

    def flip_core(x):
        return lax.ppermute(x, "blk", [(i, i ^ 1) for i in range(blk)])

    masks = tile_mask.reshape(leaves)
    total = base + width + 4 * leaves
    cut = base // 2 + width // 8
    call = functools.partial(pl.pallas_call, cost_estimate=NO_COST, compiler_params=pltpu.CompilerParams(vmem_limit_bytes=16 * MIB))
    struct = jax.ShapeDtypeStruct
    bundle = call(
        functools.partial(start_kernel, leaves, width),
        out_shape=struct((total, cols), BF16),
        in_specs=[SM, SM, SM, VM, VM, VM],
        out_specs=VM,
        scratch_shapes=[pltpu.VMEM((4 * leaves, cols), F32)],
    )(info, masks, parent, link, leaf_inverse, leaf_rhs)
    parts = [5 * base // 8, 3 * base // 8]
    solved = call(
        functools.partial(solved_kernel, leaves, width),
        out_shape=[struct((rows, cols), BF16) for rows in parts],
        in_specs=[VM, VM],
        out_specs=[VM] * len(parts),
    )(leaf_inverse, bundle)
    gathered = [lax.all_gather(part, "blk") for part in solved]

    bx, by = over_scen(bundle, 1), over_scen(bundle, 2)
    da, db = over_scen(bx[:cut], 2), over_scen(by[cut:], 1)
    tops = [bx[base:], by[base:], db[base - cut:]]
    swap = flip_core(jnp.concatenate([t[:width] for t in tops[:2]], axis=0))
    swap3 = flip_core(tops[2][:width])
    notes = [t[width:, :width].astype(F32) for t in tops]
    owners = [parent] + [n[3 * leaves:, 0].astype(jnp.int32) for n in notes]
    parents = jnp.concatenate(owners)
    sides = [leaf_rhs] + [n[:leaves] + n[leaves:2 * leaves] + n[2 * leaves:3 * leaves] for n in notes]
    rights, rights3 = jnp.concatenate(sides[:3], axis=0), jnp.concatenate(sides, axis=0)

    count = scen * leaves
    node_shape, part_shape = pltpu.VMEM((nodes, cols), F32), pltpu.VMEM((count, width), F32)
    early_shape, late_shape = pltpu.VMEM((3 * base, cols), BF16), pltpu.VMEM((base, cols), BF16)
    terms_shape = pltpu.VMEM((3 * nodes, cols), F32)
    *m_all, km_all, diag, right = call(
        functools.partial(early_kernel, leaves, width, nodes),
        out_shape=[late_shape] * 3 + [early_shape, terms_shape, terms_shape],
        in_specs=[SM, SM] + [VM] * 6,
        out_specs=[VM] * 6,
        compiler_params=pltpu.CompilerParams(vmem_limit_bytes=16 * MIB),
    )(info, jnp.concatenate(owners[:3]), rights, leaf_inverse, bundle, bx, by, swap)
    def to_columns(gathered, ties):
        *blocks, token = pick(info, [1 + k for k in (1, 2, 3)], gathered, ties)
        return [over_scen(x, k + 1) for k, x in enumerate(blocks)], token

    m3, km3, reduced, scaling, current, part = call(
        functools.partial(late_kernel, leaves, width, cut),
        out_shape=[late_shape, late_shape, node_shape, node_shape, node_shape, part_shape],
        in_specs=[SM, SM] + [VM] * 9,
        out_specs=[VM] * 6,
        compiler_params=pltpu.CompilerParams(vmem_limit_bytes=16 * MIB),
    )(info, parents, rights3, node_rhs, node_diag, da, db, swap3, in_vmem(km_all), diag, right)

    def exchange(x, tie=None):
        x = x + flip_core(x)
        other = flip_z(x, 1)
        x = x + other if tie is None else call(
            add_kernel, out_shape=pltpu.VMEM(x.shape, F32), in_specs=[VM] * 3, out_specs=VM)(x, other, tie)
        return x, flip_z(x, 2)

    def product(terms, sources, tie, acc=None, side=None, schur=None):
        held = [term for term in terms if term[2] is not None]
        dynamic = {term[1] for term in held}
        extra = [tie] + ([] if acc is None else [in_vmem(acc)]) + ([] if schur is None else [schur])
        first = 6 + len(sources)
        aliases = {} if acc is None else {first + 1: 0}
        if schur is not None:
            aliases[first + 2] = 2
        return call(
            functools.partial(product_kernel, leaves, width, terms, len(sources), acc is None, side),
            out_shape=[pltpu.VMEM((nodes, cols, cols), F32), pltpu.VMEM((8, 128), F32)]
            + ([] if side is None else [struct((nodes, cols, 2 * cols), F32)]),
            in_specs=[SM, SM] + [VM] * 4 + [HB if n in dynamic else VM for n in range(len(sources))]
            + [VM] * (1 + (acc is not None)) + [HB] * (schur is not None),
            out_specs=[VM, VM] + [HB] * (side is not None),
            scratch_shapes=[pltpu.VMEM((max(sum(term[-1] for term in held), 16), cols), BF16),
                            pltpu.SemaphoreType.DMA((max(len(held), 1),)), pltpu.SemaphoreType.DMA((4 * nodes,))],
            input_output_aliases=aliases,
            cost_estimate=pl.CostEstimate(flops=2 * sum(term[-1] for term in terms) * cols * cols, bytes_accessed=2 * MIB,
                                          transcendentals=0),
        )(info, parents, *map(in_vmem, (*m_all, m3)), *sources, *extra)

    def line_terms(side):
        return [(0, 0, 1 + side * scen, 0, 0, parts[0]), (0, 1, 1 + side * scen, 0, parts[0], parts[1])]

    own = [in_hbm(x) for x in gathered]
    first, token = to_columns(gathered[0], [part])
    arrived = exchange(part, token)
    ties = []
    for sweep in range(ITERS):
        last = sweep == ITERS - 1
        current, part = call(
            functools.partial(sweep_kernel, leaves, width, last, len(ties)),
            out_shape=[struct((nodes, cols), F32), pltpu.VMEM((leaves, width), F32)] if last else [node_shape, part_shape],
            in_specs=[SM] + [VM] * 12 + [VM if tie.dtype == F32 else HB for tie in ties],
            out_specs=[VM] * 2,
            compiler_params=pltpu.CompilerParams(vmem_limit_bytes=16 * MIB),
        )(parents, *arrived, reduced, scaling, node_diag, current, *map(in_vmem, (*m_all, m3, km_all, km3)), *ties)
        ties = []
        if sweep == 2:
            second, token = to_columns(gathered[1], [part])
            arrived = exchange(part, token)
            others = [flip_core(join(first, arrived[0]))]
            terms = line_terms(0) + [(k, 1 + k, None, 0, 0, parts[0]) for k in (1, 2, 3)]
            acc0, token = product(terms, own + first, arrived[0])
            ties = [token]
        elif last:
            terms = line_terms(1) + [(k, 2, None, (k - 1) * parts[0], 0, parts[0]) for k in (1, 2, 3)]
            acc1, token = product(terms, own + others, part)
            arrived = exchange(part, token)
            others = [flip_core(join(second, arrived[0]))]
            terms = [(k, k - 1, None, 0, parts[0], parts[1]) for k in (1, 2, 3)]
            unused, token, schur = product(terms, second, arrived[0], acc0, 0)
            ties = [token]
        else:
            arrived = exchange(part)
    leaf_solution = call(
        functools.partial(leaf_kernel, leaves),
        out_shape=struct((leaves, width), F32),
        in_specs=[VM] * 4 + [VM if tie.dtype == F32 else HB for tie in ties],
        out_specs=VM,
    )(*arrived, leaf_rhs, leaf_inverse, *ties)

    terms = [(k, 0, None, (k - 1) * parts[1], parts[0], parts[1]) for k in (1, 2, 3)]
    unused, token, schur = product(terms, others, leaf_solution, acc1, 1, schur)
    return current, leaf_solution, schur


def solution(mesh):
    scen, blk = mesh.shape["scen"], mesh.shape["blk"]
    in_specs = (
        P("scen", None, "blk"),
        P("scen", None, None),
        P("scen", None),
        P(None, "blk"),
        P(None, "blk"),
        P("scen"),
        P("scen", "blk"),
    )
    out_specs = (P(None, "blk"), P("scen", None), P(None, "blk", "scen"))
    body = functools.partial(plane_body, scen, blk) if scen == 4 and blk == 2 * scen else general_body
    return jax.shard_map(body, mesh=mesh, in_specs=in_specs, out_specs=out_specs, check_vma=False)
```

```python
import functools

import jax
import jax.numpy as jnp
from jax import lax
from jax.experimental import pallas as pl
from jax.experimental.pallas import tpu as pltpu
from jax.sharding import PartitionSpec as P

ITERS = 4
highest = lax.Precision.HIGHEST
damping = 0.4
F32 = jnp.float32
BF16 = jnp.bfloat16
MIB = 1 << 20

VM = pl.BlockSpec(memory_space=pltpu.VMEM)
SM = pl.BlockSpec(memory_space=pltpu.SMEM)
HB = pl.BlockSpec(memory_space=pltpu.HBM)
NO_COST = pl.CostEstimate(flops=0, bytes_accessed=0, transcendentals=0)


def general_body(link, leaf_inverse, leaf_rhs, node_rhs, node_diag, parent, tile_mask):
    leaf_count, width_leaf, tile_width = link.shape
    node_count = node_rhs.shape[0]
    blk_index = lax.axis_index("blk")
    node_ids = lax.broadcasted_iota(jnp.int32, (leaf_count, node_count), 1)
    member = parent[:, None] == node_ids
    member_f = member.astype(F32)
    masked = link * tile_mask.astype(BF16)[:, :, None]
    solved = jnp.einsum("lnm,lmc->lnc", leaf_inverse, masked, preferred_element_type=F32).astype(BF16)
    chosen = masked[None] * member.astype(BF16).T[:, :, None, None]
    chosen = chosen.reshape(node_count, leaf_count * width_leaf, tile_width)
    portion = lax.all_gather(solved, "blk", axis=2, tiled=True)
    stacked = portion.reshape(leaf_count * width_leaf, portion.shape[2])
    partial_value = jnp.einsum("pkr,kc->prc", chosen, stacked, preferred_element_type=F32)
    diagonal_tile = lax.dynamic_slice_in_dim(partial_value, blk_index * tile_width, tile_width, 2)
    diag_terms = jnp.diagonal(diagonal_tile, axis1=1, axis2=2)
    inverse_f = leaf_inverse.astype(F32)
    masked_f = masked.astype(F32)
    leaf_solve = jnp.einsum("lnm,lm->ln", inverse_f, leaf_rhs, precision=highest)
    leaf_terms = jnp.einsum("lnc,ln->lc", masked_f, leaf_solve, precision=highest)
    rhs_terms = jnp.dot(member_f.T, leaf_terms, precision=highest)
    rhs_sum, diag_sum = lax.psum((rhs_terms, diag_terms), "scen")
    reduced = node_rhs - rhs_sum
    scaling = node_diag + diag_sum
    schur_rows = lax.psum_scatter(partial_value, "scen", scatter_dimension=1, tiled=True)
    schur_out = lax.all_to_all(schur_rows, "scen", split_axis=2, concat_axis=1, tiled=True)
    solved_f = solved.astype(F32)
    current = reduced / scaling
    for sweep in range(ITERS):
        parent_tile = jnp.dot(member_f, current, precision=highest)
        local_image = jnp.einsum("lnc,lc->ln", solved_f, parent_tile, precision=highest)
        leaf_image = lax.psum(local_image, "blk")
        spread = jnp.einsum("lnc,ln->lc", masked_f, leaf_image, precision=highest)
        node_terms = jnp.dot(member_f.T, spread, precision=highest)
        coupled = lax.psum(node_terms, "scen")
        product = node_diag * current + coupled
        current = current + damping * (reduced - product) / scaling
    parent_values = jnp.dot(member_f, current, precision=highest)
    link_term = jnp.einsum("lnc,lc->ln", masked_f, parent_values, precision=highest)
    summed = lax.psum(link_term, "blk")
    leaf_solution = jnp.einsum("lnm,lm->ln", inverse_f, leaf_rhs - summed, precision=highest)
    return (current, leaf_solution, schur_out)


def split3(x):
    hi = x.astype(BF16)
    rest = x - hi.astype(F32)
    mid = rest.astype(BF16)
    low = (rest - mid.astype(F32)).astype(BF16)
    row = lax.broadcasted_iota(jnp.int32, (8, x.shape[1]), 0)
    wide = lambda v: jnp.broadcast_to(v.astype(F32), (8, x.shape[1]))
    out = jnp.where(row == 0, wide(hi), jnp.where(row == 1, wide(mid), jnp.where(row == 2, wide(low), 0.0)))
    return out.astype(BF16)


def rowdot(x, mat, transposed):
    dims = (((1,), (1 if transposed else 0,)), ((), ()))
    return jnp.sum(lax.dot_general(split3(x), mat, dims, preferred_element_type=F32), axis=0, keepdims=True)


def start_kernel(leaves, width, core_ref, mask_ref, parent_ref, link_ref, inverse_ref, rhs_ref, bundle_ref, notes_ref):
    half = leaves // 2
    base = leaves * width
    for i in range(half):
        bundle_ref[pl.ds(base, width), pl.ds(i * width, width)] = inverse_ref[core_ref[0] * half + i]
    notes_ref[...] = jnp.zeros_like(notes_ref)
    value = rhs_ref[...]
    for n in range(3):
        term = value.astype(BF16).astype(F32)
        notes_ref[pl.ds(n * leaves, leaves), pl.ds(0, width)] = term
        value = value - term
    for l in range(leaves):
        notes_ref[pl.ds(3 * leaves + l, 1), :] = jnp.full((1, notes_ref.shape[1]), parent_ref[l].astype(F32))
    bundle_ref[pl.ds(base + width, 4 * leaves), :] = notes_ref[...].astype(BF16)
    for l in range(leaves):
        bundle_ref[pl.ds(l * width, width), :] = masked_tile(mask_ref, link_ref, l)


def masked_tile(mask_ref, link_ref, l):
    return jnp.where(mask_ref[l] != 0, link_ref[l].astype(F32), 0.0).astype(BF16)


def solved_kernel(leaves, width, inverse_ref, bundle_ref, *refs):
    for l in range(leaves):
        tile = bundle_ref[pl.ds(l * width, width), :]
        solved = jnp.dot(inverse_ref[l], tile, preferred_element_type=F32).astype(BF16)
        start = 0
        for ref in refs:
            low, high = max(l * width, start), min((l + 1) * width, start + ref.shape[0])
            if low < high:
                ref[pl.ds(low - start, high - low), :] = solved[low - l * width:high - l * width]
            start += ref.shape[0]


def node_add(acc, parent, value):
    return [jnp.where(parent == p, a + value, a) for p, a in enumerate(acc)]


def tree(groups):
    while len(groups) > 1:
        groups = [[a + b for a, b in zip(groups[i], groups[i + 1])] for i in range(0, len(groups), 2)]
    return groups[0]


def stack3(values):
    count = -(-3 * len(values) // 8) * 8
    row = lax.broadcasted_iota(jnp.int32, (count, values[0].shape[1]), 0)
    out = jnp.zeros(row.shape, F32)
    for p, value in enumerate(values):
        for j in range(3):
            term = value.astype(BF16).astype(F32)
            out = jnp.where(row == 3 * p + j, jnp.broadcast_to(term, row.shape), out)
            value = value - term
    return out.astype(BF16)


def unstack3(out, count):
    return [out[3 * p:3 * p + 1] + out[3 * p + 1:3 * p + 2] + out[3 * p + 2:3 * p + 3] for p in range(count)]


def spread_group(leaves, width, first, whole, mat, parent_ref, nodes):
    values = [jnp.concatenate([jnp.where(parent_ref[first + i] == p, whole[first + i:first + i + 1, :], 0.0) for i in range(leaves)],
                              axis=1) for p in range(nodes)]
    return unstack3(jnp.dot(stack3(values), mat, preferred_element_type=F32), nodes)


def image_group(leaves, width, first, mat, stacked, nodes, parent_ref, part_ref):
    out = unstack3(lax.dot_general(stacked, mat, (((1,), (1,)), ((), ())), preferred_element_type=F32), nodes)
    for i in range(leaves):
        lanes = slice(i * width, (i + 1) * width)
        value = out[0][:, lanes]
        for p in range(1, nodes):
            value = jnp.where(parent_ref[first + i] == p, out[p][:, lanes], value)
        part_ref[pl.ds(first + i, 1), :] = value


def group_work(leaves, width, first_leaf, group, tile_of, inv_of, m_ref, km_ref, rhs_ref, parent_ref, nodes, cols):
    zero = jnp.zeros((1, cols), F32)
    diag, right = [zero] * nodes, [zero] * nodes
    for i in range(leaves):
        l = first_leaf + i
        rows = pl.ds((group * leaves + i) * width, width)
        inv, tile = inv_of(i), tile_of(i)
        m_ref[pl.ds(i * width, width), :] = tile
        solved = jnp.dot(inv, tile, preferred_element_type=F32).astype(BF16)
        km_ref[rows, :] = solved
        p = parent_ref[l]
        diag = node_add(diag, p, jnp.sum(tile.astype(F32) * solved.astype(F32), axis=0, keepdims=True))
        leaf = rowdot(rhs_ref[pl.ds(l, 1), :], inv, True)
        right = node_add(right, p, rowdot(leaf, tile, False))
    return diag, right


def tile_in(leaves, width, cut, top_ref, end_ref):
    def tile(i):
        top = min(max(cut - i * width, 0), width)
        parts = []
        if top:
            parts.append(top_ref[pl.ds(i * width, top), :])
        if top < width:
            parts.append(end_ref[pl.ds(i * width + top - cut, width - top), :])
        return parts[0] if len(parts) == 1 else jnp.concatenate(parts, axis=0)
    return tile


def pair_in(leaves, width, core_ref, own, other):
    first = core_ref[0] == 0
    own, other = own.astype(F32), other.astype(F32)
    pair = [jnp.where(first, own, other).astype(BF16), jnp.where(first, other, own).astype(BF16)]
    def inv(i):
        h, j = divmod(i, leaves // 2)
        return pair[h][:, j * width:(j + 1) * width]
    return inv


def early_kernel(leaves, width, nodes, core_ref, parent_ref, rhs_ref, inverse_ref, own_ref, x_ref, y_ref, swap_ref, *refs):
    m_refs, (km_ref, diag_ref, right_ref) = refs[:3], refs[3:]
    base, cols = leaves * width, own_ref.shape[1]
    for k, ref in enumerate((own_ref, x_ref, y_ref)):
        if k:
            inv = pair_in(leaves, width, core_ref, ref[pl.ds(base, width), :], swap_ref[pl.ds((k - 1) * width, width), :])
        else:
            inv = lambda i: inverse_ref[i]
        tile = lambda i: ref[pl.ds(i * width, width), :]
        diag, right = group_work(leaves, width, k * leaves, k, tile, inv, m_refs[k], km_ref, rhs_ref, parent_ref, nodes, cols)
        for p in range(nodes):
            diag_ref[pl.ds(k * nodes + p, 1), :] = diag[p]
            right_ref[pl.ds(k * nodes + p, 1), :] = right[p]


def late_kernel(leaves, width, cut, core_ref, parent_ref, rhs_ref, node_rhs_ref, node_diag_ref, da_ref, db_ref, swap_ref, early_ref,
                diag_ref, right_ref, m_ref, km_ref, reduced_ref, scaling_ref, x_ref, part_ref):
    nodes, cols = node_rhs_ref.shape
    base = leaves * width
    inv = pair_in(leaves, width, core_ref, db_ref[pl.ds(base - cut, width), :], swap_ref[...])
    diag, right = group_work(leaves, width, 3 * leaves, 0, tile_in(leaves, width, cut, da_ref, db_ref), inv, m_ref, km_ref, rhs_ref,
                             parent_ref, nodes, cols)
    rows = lambda ref: [[ref[pl.ds(k * nodes + p, 1), :] for p in range(nodes)] for k in range(3)]
    diag, right = tree(rows(diag_ref) + [diag]), tree(rows(right_ref) + [right])
    start = []
    for p in range(nodes):
        at = pl.ds(p, 1)
        reduced = node_rhs_ref[at, :] - right[p]
        scaling = node_diag_ref[at, :] + diag[p]
        reduced_ref[at, :] = reduced
        scaling_ref[at, :] = scaling
        start.append(reduced / scaling)
        x_ref[at, :] = start[p]
    image(leaves, width, early_ref, km_ref, start, parent_ref, part_ref)


def image(leaves, width, early_ref, late_ref, values, parent_ref, part_ref):
    stacked, base = stack3(values), leaves * width
    for k in range(4):
        mat = early_ref[pl.ds(k * base, base), :] if k < 3 else late_ref[...]
        image_group(leaves, width, k * leaves, mat, stacked, len(values), parent_ref, part_ref)


def sweep_kernel(leaves, width, last, ties, parent_ref, y_ref, z_ref, reduced_ref, scaling_ref, diag_ref, x_in_ref, m0_ref, m1_ref, m2_ref, m3_ref,
                 km_ref, km3_ref, *refs):
    m_refs = (m0_ref, m1_ref, m2_ref, m3_ref)
    x_ref, part_ref = refs[ties:]
    nodes = x_in_ref.shape[0]
    whole = y_ref[...] + z_ref[...]
    groups = [spread_group(leaves, width, k * leaves, whole, m_refs[k][...], parent_ref, nodes) for k in range(4)]
    coupled = tree(groups)
    new = []
    for p in range(nodes):
        at = pl.ds(p, 1)
        x = x_in_ref[at, :]
        x = x + damping * (reduced_ref[at, :] - diag_ref[at, :] * x - coupled[p]) / scaling_ref[at, :]
        x_ref[at, :] = x
        new.append(x)
    if last:
        image_group(leaves, width, 0, m_refs[0][...], stack3(new), nodes, parent_ref, part_ref)
    else:
        image(leaves, width, km_ref, km3_ref, new, parent_ref, part_ref)


def add_kernel(x_ref, y_ref, tie_ref, out_ref):
    del tie_ref
    out_ref[...] = x_ref[...] + y_ref[...]


def leaf_kernel(leaves, y_ref, z_ref, rhs_ref, inverse_ref, *refs):
    out_ref = refs[-1]
    rest = rhs_ref[...] - (y_ref[...] + z_ref[...])
    for l in range(leaves):
        out_ref[pl.ds(l, 1), :] = rowdot(rest[l:l + 1, :], inverse_ref[l], True)


def join(blocks, tie):
    rows = blocks[0].shape[0]

    def kernel(*refs):
        out_ref = refs[-1]
        for n in range(len(blocks)):
            out_ref[pl.ds(n * rows, rows), :] = refs[n][...]

    return pl.pallas_call(
        kernel,
        out_shape=jax.ShapeDtypeStruct((len(blocks) * rows, blocks[0].shape[1]), blocks[0].dtype),
        in_specs=[VM] * (len(blocks) + 1),
        out_specs=VM,
        compiler_params=pltpu.CompilerParams(vmem_limit_bytes=16 * MIB),
        cost_estimate=NO_COST,
    )(*blocks, tie)


def in_vmem(x):
    return pltpu.with_memory_space_constraint(x, pltpu.VMEM)


def in_hbm(x):
    return pltpu.with_memory_space_constraint(x, pltpu.HBM)


def pick(info, places, source, ties):
    shape = jax.ShapeDtypeStruct(source.shape[1:], source.dtype)
    count = len(places)

    def kernel(place_ref, source_ref, *refs):
        first = len(ties)
        outs, token_ref = refs[first:first + count], refs[first + count]
        held, sem_in, sem_out = refs[first + count + 1:]
        token_ref[...] = jnp.zeros_like(token_ref)
        reads = [pltpu.make_async_copy(source_ref.at[place_ref[places[n]]], held.at[n], sem_in.at[n]) for n in range(count)]
        writes = [pltpu.make_async_copy(held.at[n], outs[n], sem_out.at[n]) for n in range(count)]
        for read in reads:
            read.start()
        for read, write in zip(reads, writes):
            read.wait()
            write.start()
        for write in writes:
            write.wait()

    return pl.pallas_call(
        kernel,
        out_shape=[shape] * count + [jax.ShapeDtypeStruct((8, 128), F32)],
        in_specs=[SM, HB] + [VM] * len(ties),
        out_specs=[HB] * count + [VM],
        scratch_shapes=[pltpu.VMEM((count,) + shape.shape, shape.dtype), pltpu.SemaphoreType.DMA((count,)),
                        pltpu.SemaphoreType.DMA((count,))],
        compiler_params=pltpu.CompilerParams(vmem_limit_bytes=12 * MIB),
        cost_estimate=NO_COST,
    )(info, in_hbm(source), *ties)


def leaf_spans(width, start, rows):
    spans = []
    while rows:
        size = min(rows, width - start % width)
        spans.append((start // width, start, size))
        start, rows = start + size, rows - size
    return spans


def product_kernel(leaves, width, terms, count, fresh, side, info_ref, parent_ref, *refs):
    m_refs, sources = refs[:4], refs[4:4 + count]
    outs, (u_ref, sem, out_sem) = refs[:-3][-2 - (side is not None):], refs[-3:]
    acc_ref, token_ref = outs[:2]
    work, late, slot = [], [], 0
    for k, n, entry, offset, start, rows in terms:
        if entry is None:
            ref, offset = sources[n], offset
        else:
            copy = pltpu.make_async_copy(sources[n].at[info_ref[entry]], u_ref.at[pl.ds(slot, rows)], sem.at[len(late)])
            copy.start()
            late.append(copy)
            ref, offset = u_ref, slot
            slot += rows
        spans = [(k, leaf, at, ref, offset + at - start, size) for leaf, at, size in leaf_spans(width, start, rows)]
        work = work + spans if entry is not None else spans + work
    token_ref[...] = jnp.zeros_like(token_ref)
    if fresh:
        acc_ref[...] = jnp.zeros_like(acc_ref)
    for k, leaf, at, ref, offset, size in work:
        if ref is u_ref:
            for copy in late:
                copy.wait()
            late = []
        value = lax.dot_general(m_refs[k][pl.ds(at, size), :], ref[pl.ds(offset, size), :], (((0,), (0,)), ((), ())),
                                preferred_element_type=F32)
        acc_ref[parent_ref[k * leaves + leaf]] += value
    if side is not None:
        nodes, rows, cols = acc_ref.shape
        where = info_ref[0] if side == 0 else 1 - info_ref[0]
        size = rows // 4
        pieces = [(p, pl.ds(i * size, size)) for p in range(nodes) for i in range(4)]
        for half in range(2):
            @pl.when(where == half)
            def _():
                for n, (p, at) in enumerate(pieces):
                    pltpu.make_async_copy(acc_ref.at[p, at], outs[2].at[p, at, pl.ds(half * cols, cols)], out_sem.at[n]).start()
        for n, (p, at) in enumerate(pieces):
            pltpu.make_async_copy(acc_ref.at[p, at], outs[2].at[p, at, pl.ds(0, cols)], out_sem.at[n]).wait()


def plane_body(scen, blk, link, leaf_inverse, leaf_rhs, node_rhs, node_diag, parent, tile_mask):
    leaves, width, cols = link.shape
    nodes = node_rhs.shape[0]
    base = leaves * width
    planes = blk // 2
    s, b = lax.axis_index("scen"), lax.axis_index("blk")
    z, core = b // 2, b % 2
    info = jnp.stack([core] + [2 * (s ^ k) + c for c in (core, 1 - core) for k in range(scen)]).astype(jnp.int32)

    def over_scen(x, k):
        return lax.ppermute(x, "scen", [(i, i ^ k) for i in range(scen)])

    def flip_z(x, k):
        return lax.ppermute(x, "blk", [(i, i ^ (2 * k)) for i in range(blk)])

    def flip_core(x):
        return lax.ppermute(x, "blk", [(i, i ^ 1) for i in range(blk)])

    masks = tile_mask.reshape(leaves)
    total = base + width + 4 * leaves
    cut = base // 2 + width // 8
    call = functools.partial(pl.pallas_call, cost_estimate=NO_COST, compiler_params=pltpu.CompilerParams(vmem_limit_bytes=16 * MIB))
    struct = jax.ShapeDtypeStruct
    bundle = call(
        functools.partial(start_kernel, leaves, width),
        out_shape=struct((total, cols), BF16),
        in_specs=[SM, SM, SM, VM, VM, VM],
        out_specs=VM,
        scratch_shapes=[pltpu.VMEM((4 * leaves, cols), F32)],
    )(info, in_hbm(masks), in_hbm(parent), in_hbm(link), in_hbm(leaf_inverse), in_hbm(leaf_rhs))
    parts = [5 * base // 8, 3 * base // 8]
    solved = call(
        functools.partial(solved_kernel, leaves, width),
        out_shape=[struct((rows, cols), BF16) for rows in parts],
        in_specs=[VM, VM],
        out_specs=[VM] * len(parts),
    )(in_hbm(leaf_inverse), bundle)
    gathered = [lax.all_gather(part, "blk") for part in solved]

    bx, by = over_scen(bundle, 1), over_scen(bundle, 2)
    da, db = over_scen(bx[:cut], 2), over_scen(by[cut:], 1)
    tops = [bx[base:], by[base:], db[base - cut:]]
    swap = flip_core(jnp.concatenate([t[:width] for t in tops[:2]], axis=0))
    swap3 = flip_core(tops[2][:width])
    notes = [t[width:, :width].astype(F32) for t in tops]
    owners = [parent] + [n[3 * leaves:, 0].astype(jnp.int32) for n in notes]
    parents = jnp.concatenate(owners)
    sides = [leaf_rhs] + [n[:leaves] + n[leaves:2 * leaves] + n[2 * leaves:3 * leaves] for n in notes]
    rights, rights3 = jnp.concatenate(sides[:3], axis=0), jnp.concatenate(sides, axis=0)

    count = scen * leaves
    node_shape, part_shape = pltpu.VMEM((nodes, cols), F32), pltpu.VMEM((count, width), F32)
    early_shape, late_shape = pltpu.VMEM((3 * base, cols), BF16), pltpu.VMEM((base, cols), BF16)
    terms_shape = pltpu.VMEM((3 * nodes, cols), F32)
    *m_all, km_all, diag, right = call(
        functools.partial(early_kernel, leaves, width, nodes),
        out_shape=[late_shape] * 3 + [early_shape, terms_shape, terms_shape],
        in_specs=[SM, SM] + [VM] * 6,
        out_specs=[VM] * 6,
        compiler_params=pltpu.CompilerParams(vmem_limit_bytes=16 * MIB),
    )(info, jnp.concatenate(owners[:3]), rights, leaf_inverse, bundle, bx, by, swap)
    def to_columns(gathered, ties):
        *blocks, token = pick(info, [1 + k for k in (1, 2, 3)], gathered, ties)
        return [over_scen(x, k + 1) for k, x in enumerate(blocks)], token

    m3, km3, reduced, scaling, current, part = call(
        functools.partial(late_kernel, leaves, width, cut),
        out_shape=[pltpu.HBM((base, cols), BF16)] * 2 + [node_shape, node_shape, node_shape, part_shape],
        in_specs=[SM, SM] + [VM] * 9,
        out_specs=[VM] * 6,
        compiler_params=pltpu.CompilerParams(vmem_limit_bytes=16 * MIB),
    )(info, parents, rights3, node_rhs, node_diag, da, db, swap3, in_vmem(km_all), diag, right)

    def exchange(x, tie=None):
        x = x + flip_core(x)
        other = flip_z(x, 1)
        x = x + other if tie is None else call(
            add_kernel, out_shape=pltpu.VMEM(x.shape, F32), in_specs=[VM] * 3, out_specs=VM)(x, other, tie)
        return x, flip_z(x, 2)

    def product(terms, sources, tie, acc=None, side=None, schur=None):
        held = [term for term in terms if term[2] is not None]
        dynamic = {term[1] for term in held}
        extra = [tie] + ([] if acc is None else [in_vmem(acc)]) + ([] if schur is None else [schur])
        first = 6 + len(sources)
        aliases = {} if acc is None else {first + 1: 0}
        if schur is not None:
            aliases[first + 2] = 2
        return call(
            functools.partial(product_kernel, leaves, width, terms, len(sources), acc is None, side),
            out_shape=[pltpu.VMEM((nodes, cols, cols), F32), pltpu.VMEM((8, 128), F32)]
            + ([] if side is None else [struct((nodes, cols, 2 * cols), F32)]),
            in_specs=[SM, SM] + [VM] * 4 + [HB if n in dynamic else VM for n in range(len(sources))]
            + [VM] * (1 + (acc is not None)) + [HB] * (schur is not None),
            out_specs=[VM, VM] + [HB] * (side is not None),
            scratch_shapes=[pltpu.VMEM((max(sum(term[-1] for term in held), 16), cols), BF16),
                            pltpu.SemaphoreType.DMA((max(len(held), 1),)), pltpu.SemaphoreType.DMA((4 * nodes,))],
            input_output_aliases=aliases,
            cost_estimate=pl.CostEstimate(flops=2 * sum(term[-1] for term in terms) * cols * cols, bytes_accessed=2 * MIB,
                                          transcendentals=0),
        )(info, parents, *map(in_vmem, (*m_all, m3)), *sources, *extra)

    def line_terms(side):
        return [(0, 0, 1 + side * scen, 0, 0, parts[0]), (0, 1, 1 + side * scen, 0, parts[0], parts[1])]

    own = [in_hbm(x) for x in gathered]
    first, token = to_columns(gathered[0], [part])
    arrived = exchange(part, token)
    ties = []
    for sweep in range(ITERS):
        last = sweep == ITERS - 1
        current, part = call(
            functools.partial(sweep_kernel, leaves, width, last, len(ties)),
            out_shape=[struct((nodes, cols), F32), pltpu.VMEM((leaves, width), F32)] if last else [node_shape, part_shape],
            in_specs=[SM] + [VM] * 12 + [VM if tie.dtype == F32 else HB for tie in ties],
            out_specs=[VM] * 2,
            compiler_params=pltpu.CompilerParams(vmem_limit_bytes=16 * MIB),
        )(parents, *arrived, reduced, scaling, node_diag, current, *map(in_vmem, (*m_all, m3, km_all, km3)), *ties)
        ties = []
        if sweep == 2:
            second, token = to_columns(gathered[1], [part])
            arrived = exchange(part, token)
            others = [flip_core(join(first, arrived[0]))]
            terms = line_terms(0) + [(k, 1 + k, None, 0, 0, parts[0]) for k in (1, 2, 3)]
            acc0, token = product(terms, own + first, arrived[0])
            ties = [token]
        elif last:
            terms = line_terms(1) + [(k, 2, None, (k - 1) * parts[0], 0, parts[0]) for k in (1, 2, 3)]
            acc1, token = product(terms, own + others, part)
            arrived = exchange(part, token)
            others = [flip_core(join(second, arrived[0]))]
            terms = [(k, k - 1, None, 0, parts[0], parts[1]) for k in (1, 2, 3)]
            unused, token, schur = product(terms, second, arrived[0], acc0, 0)
            ties = [token]
        else:
            arrived = exchange(part)
    leaf_solution = call(
        functools.partial(leaf_kernel, leaves),
        out_shape=struct((leaves, width), F32),
        in_specs=[VM] * 4 + [VM if tie.dtype == F32 else HB for tie in ties],
        out_specs=VM,
    )(*arrived, leaf_rhs, leaf_inverse, *ties)

    terms = [(k, 0, None, (k - 1) * parts[1], parts[0], parts[1]) for k in (1, 2, 3)]
    unused, token, schur = product(terms, others, leaf_solution, acc1, 1, schur)
    return current, leaf_solution, schur


def solution(mesh):
    scen, blk = mesh.shape["scen"], mesh.shape["blk"]
    in_specs = (
        P("scen", None, "blk"),
        P("scen", None, None),
        P("scen", None),
        P(None, "blk"),
        P(None, "blk"),
        P("scen"),
        P("scen", "blk"),
    )
    out_specs = (P(None, "blk"), P("scen", None), P(None, "blk", "scen"))
    body = functools.partial(plane_body, scen, blk) if scen == 4 and blk == 2 * scen else general_body
    return jax.shard_map(body, mesh=mesh, in_specs=in_specs, out_specs=out_specs, check_vma=False)
```

```python
import functools

import jax
import jax.numpy as jnp
from jax import lax
from jax.experimental import pallas as pl
from jax.experimental.pallas import tpu as pltpu
from jax.sharding import PartitionSpec as P

ITERS = 4
highest = lax.Precision.HIGHEST
damping = 0.4
F32 = jnp.float32
BF16 = jnp.bfloat16
MIB = 1 << 20

VM = pl.BlockSpec(memory_space=pltpu.VMEM)
SM = pl.BlockSpec(memory_space=pltpu.SMEM)
HB = pl.BlockSpec(memory_space=pltpu.HBM)
NO_COST = pl.CostEstimate(flops=0, bytes_accessed=0, transcendentals=0)


def general_body(link, leaf_inverse, leaf_rhs, node_rhs, node_diag, parent, tile_mask):
    leaf_count, width_leaf, tile_width = link.shape
    node_count = node_rhs.shape[0]
    blk_index = lax.axis_index("blk")
    node_ids = lax.broadcasted_iota(jnp.int32, (leaf_count, node_count), 1)
    member = parent[:, None] == node_ids
    member_f = member.astype(F32)
    masked = link * tile_mask.astype(BF16)[:, :, None]
    solved = jnp.einsum("lnm,lmc->lnc", leaf_inverse, masked, preferred_element_type=F32).astype(BF16)
    chosen = masked[None] * member.astype(BF16).T[:, :, None, None]
    chosen = chosen.reshape(node_count, leaf_count * width_leaf, tile_width)
    portion = lax.all_gather(solved, "blk", axis=2, tiled=True)
    stacked = portion.reshape(leaf_count * width_leaf, portion.shape[2])
    partial_value = jnp.einsum("pkr,kc->prc", chosen, stacked, preferred_element_type=F32)
    diagonal_tile = lax.dynamic_slice_in_dim(partial_value, blk_index * tile_width, tile_width, 2)
    diag_terms = jnp.diagonal(diagonal_tile, axis1=1, axis2=2)
    inverse_f = leaf_inverse.astype(F32)
    masked_f = masked.astype(F32)
    leaf_solve = jnp.einsum("lnm,lm->ln", inverse_f, leaf_rhs, precision=highest)
    leaf_terms = jnp.einsum("lnc,ln->lc", masked_f, leaf_solve, precision=highest)
    rhs_terms = jnp.dot(member_f.T, leaf_terms, precision=highest)
    rhs_sum, diag_sum = lax.psum((rhs_terms, diag_terms), "scen")
    reduced = node_rhs - rhs_sum
    scaling = node_diag + diag_sum
    schur_rows = lax.psum_scatter(partial_value, "scen", scatter_dimension=1, tiled=True)
    schur_out = lax.all_to_all(schur_rows, "scen", split_axis=2, concat_axis=1, tiled=True)
    solved_f = solved.astype(F32)
    current = reduced / scaling
    for sweep in range(ITERS):
        parent_tile = jnp.dot(member_f, current, precision=highest)
        local_image = jnp.einsum("lnc,lc->ln", solved_f, parent_tile, precision=highest)
        leaf_image = lax.psum(local_image, "blk")
        spread = jnp.einsum("lnc,ln->lc", masked_f, leaf_image, precision=highest)
        node_terms = jnp.dot(member_f.T, spread, precision=highest)
        coupled = lax.psum(node_terms, "scen")
        product = node_diag * current + coupled
        current = current + damping * (reduced - product) / scaling
    parent_values = jnp.dot(member_f, current, precision=highest)
    link_term = jnp.einsum("lnc,lc->ln", masked_f, parent_values, precision=highest)
    summed = lax.psum(link_term, "blk")
    leaf_solution = jnp.einsum("lnm,lm->ln", inverse_f, leaf_rhs - summed, precision=highest)
    return (current, leaf_solution, schur_out)


def split3(x):
    hi = x.astype(BF16)
    rest = x - hi.astype(F32)
    mid = rest.astype(BF16)
    low = (rest - mid.astype(F32)).astype(BF16)
    row = lax.broadcasted_iota(jnp.int32, (8, x.shape[1]), 0)
    wide = lambda v: jnp.broadcast_to(v.astype(F32), (8, x.shape[1]))
    out = jnp.where(row == 0, wide(hi), jnp.where(row == 1, wide(mid), jnp.where(row == 2, wide(low), 0.0)))
    return out.astype(BF16)


def rowdot(x, mat, transposed):
    dims = (((1,), (1 if transposed else 0,)), ((), ()))
    return jnp.sum(lax.dot_general(split3(x), mat, dims, preferred_element_type=F32), axis=0, keepdims=True)


def start_kernel(leaves, width, core_ref, mask_ref, parent_ref, link_ref, inverse_ref, rhs_ref, bundle_ref, notes_ref):
    half = leaves // 2
    base = leaves * width
    for i in range(half):
        bundle_ref[pl.ds(base, width), pl.ds(i * width, width)] = inverse_ref[core_ref[0] * half + i]
    notes_ref[...] = jnp.zeros_like(notes_ref)
    value = rhs_ref[...]
    for n in range(3):
        term = value.astype(BF16).astype(F32)
        notes_ref[pl.ds(n * leaves, leaves), pl.ds(0, width)] = term
        value = value - term
    for l in range(leaves):
        notes_ref[pl.ds(3 * leaves + l, 1), :] = jnp.full((1, notes_ref.shape[1]), parent_ref[l].astype(F32))
    bundle_ref[pl.ds(base + width, 4 * leaves), :] = notes_ref[...].astype(BF16)
    for l in range(leaves):
        bundle_ref[pl.ds(l * width, width), :] = masked_tile(mask_ref, link_ref, l)


def masked_tile(mask_ref, link_ref, l):
    return jnp.where(mask_ref[l] != 0, link_ref[l].astype(F32), 0.0).astype(BF16)


def solved_kernel(leaves, width, inverse_ref, bundle_ref, *refs):
    for l in range(leaves):
        tile = bundle_ref[pl.ds(l * width, width), :]
        solved = jnp.dot(inverse_ref[l], tile, preferred_element_type=F32).astype(BF16)
        start = 0
        for ref in refs:
            low, high = max(l * width, start), min((l + 1) * width, start + ref.shape[0])
            if low < high:
                ref[pl.ds(low - start, high - low), :] = solved[low - l * width:high - l * width]
            start += ref.shape[0]


def node_add(acc, parent, value):
    return [jnp.where(parent == p, a + value, a) for p, a in enumerate(acc)]


def tree(groups):
    while len(groups) > 1:
        groups = [[a + b for a, b in zip(groups[i], groups[i + 1])] for i in range(0, len(groups), 2)]
    return groups[0]


def stack3(values):
    count = -(-3 * len(values) // 8) * 8
    row = lax.broadcasted_iota(jnp.int32, (count, values[0].shape[1]), 0)
    out = jnp.zeros(row.shape, F32)
    for p, value in enumerate(values):
        for j in range(3):
            term = value.astype(BF16).astype(F32)
            out = jnp.where(row == 3 * p + j, jnp.broadcast_to(term, row.shape), out)
            value = value - term
    return out.astype(BF16)


def unstack3(out, count):
    return [out[3 * p:3 * p + 1] + out[3 * p + 1:3 * p + 2] + out[3 * p + 2:3 * p + 3] for p in range(count)]


def spread_group(leaves, width, first, whole, mat, parent_ref, nodes):
    values = [jnp.concatenate([jnp.where(parent_ref[first + i] == p, whole[first + i:first + i + 1, :], 0.0) for i in range(leaves)],
                              axis=1) for p in range(nodes)]
    return unstack3(jnp.dot(stack3(values), mat, preferred_element_type=F32), nodes)


def image_group(leaves, width, first, mat, stacked, nodes, parent_ref, part_ref):
    out = unstack3(lax.dot_general(stacked, mat, (((1,), (1,)), ((), ())), preferred_element_type=F32), nodes)
    for i in range(leaves):
        lanes = slice(i * width, (i + 1) * width)
        value = out[0][:, lanes]
        for p in range(1, nodes):
            value = jnp.where(parent_ref[first + i] == p, out[p][:, lanes], value)
        part_ref[pl.ds(first + i, 1), :] = value


def group_work(leaves, width, first_leaf, group, tile_of, inv_of, m_ref, km_ref, rhs_ref, parent_ref, nodes, cols):
    zero = jnp.zeros((1, cols), F32)
    diag, right = [zero] * nodes, [zero] * nodes
    for i in range(leaves):
        l = first_leaf + i
        rows = pl.ds((group * leaves + i) * width, width)
        inv, tile = inv_of(i), tile_of(i)
        m_ref[pl.ds(i * width, width), :] = tile
        solved = jnp.dot(inv, tile, preferred_element_type=F32).astype(BF16)
        km_ref[rows, :] = solved
        p = parent_ref[l]
        diag = node_add(diag, p, jnp.sum(tile.astype(F32) * solved.astype(F32), axis=0, keepdims=True))
        leaf = rowdot(rhs_ref[pl.ds(l, 1), :], inv, True)
        right = node_add(right, p, rowdot(leaf, tile, False))
    return diag, right


def tile_in(leaves, width, cut, top_ref, end_ref):
    def tile(i):
        top = min(max(cut - i * width, 0), width)
        parts = []
        if top:
            parts.append(top_ref[pl.ds(i * width, top), :])
        if top < width:
            parts.append(end_ref[pl.ds(i * width + top - cut, width - top), :])
        return parts[0] if len(parts) == 1 else jnp.concatenate(parts, axis=0)
    return tile


def pair_in(leaves, width, core_ref, own, other):
    first = core_ref[0] == 0
    own, other = own.astype(F32), other.astype(F32)
    pair = [jnp.where(first, own, other).astype(BF16), jnp.where(first, other, own).astype(BF16)]
    def inv(i):
        h, j = divmod(i, leaves // 2)
        return pair[h][:, j * width:(j + 1) * width]
    return inv


def early_kernel(leaves, width, nodes, core_ref, parent_ref, rhs_ref, inverse_ref, own_ref, x_ref, y_ref, swap_ref, *refs):
    m_refs, (km_ref, diag_ref, right_ref) = refs[:3], refs[3:]
    base, cols = leaves * width, own_ref.shape[1]
    for k, ref in enumerate((own_ref, x_ref, y_ref)):
        if k:
            inv = pair_in(leaves, width, core_ref, ref[pl.ds(base, width), :], swap_ref[pl.ds((k - 1) * width, width), :])
        else:
            inv = lambda i: inverse_ref[i]
        tile = lambda i: ref[pl.ds(i * width, width), :]
        diag, right = group_work(leaves, width, k * leaves, k, tile, inv, m_refs[k], km_ref, rhs_ref, parent_ref, nodes, cols)
        for p in range(nodes):
            diag_ref[pl.ds(k * nodes + p, 1), :] = diag[p]
            right_ref[pl.ds(k * nodes + p, 1), :] = right[p]


def late_kernel(leaves, width, cut, core_ref, parent_ref, rhs_ref, node_rhs_ref, node_diag_ref, da_ref, db_ref, swap_ref, early_ref,
                diag_ref, right_ref, m_ref, km_ref, reduced_ref, scaling_ref, x_ref, part_ref):
    nodes, cols = node_rhs_ref.shape
    base = leaves * width
    inv = pair_in(leaves, width, core_ref, db_ref[pl.ds(base - cut, width), :], swap_ref[...])
    diag, right = group_work(leaves, width, 3 * leaves, 0, tile_in(leaves, width, cut, da_ref, db_ref), inv, m_ref, km_ref, rhs_ref,
                             parent_ref, nodes, cols)
    rows = lambda ref: [[ref[pl.ds(k * nodes + p, 1), :] for p in range(nodes)] for k in range(3)]
    diag, right = tree(rows(diag_ref) + [diag]), tree(rows(right_ref) + [right])
    start = []
    for p in range(nodes):
        at = pl.ds(p, 1)
        reduced = node_rhs_ref[at, :] - right[p]
        scaling = node_diag_ref[at, :] + diag[p]
        reduced_ref[at, :] = reduced
        scaling_ref[at, :] = scaling
        start.append(reduced / scaling)
        x_ref[at, :] = start[p]
    image(leaves, width, early_ref, km_ref, start, parent_ref, part_ref)


def image(leaves, width, early_ref, late_ref, values, parent_ref, part_ref):
    stacked, base = stack3(values), leaves * width
    for k in range(4):
        mat = early_ref[pl.ds(k * base, base), :] if k < 3 else late_ref[...]
        image_group(leaves, width, k * leaves, mat, stacked, len(values), parent_ref, part_ref)


def sweep_kernel(leaves, width, last, ties, parent_ref, y_ref, z_ref, reduced_ref, scaling_ref, diag_ref, x_in_ref, m0_ref, m1_ref, m2_ref, m3_ref,
                 km_ref, km3_ref, *refs):
    m_refs = (m0_ref, m1_ref, m2_ref, m3_ref)
    x_ref, part_ref = refs[ties:]
    nodes = x_in_ref.shape[0]
    whole = y_ref[...] + z_ref[...]
    groups = [spread_group(leaves, width, k * leaves, whole, m_refs[k][...], parent_ref, nodes) for k in range(4)]
    coupled = tree(groups)
    new = []
    for p in range(nodes):
        at = pl.ds(p, 1)
        x = x_in_ref[at, :]
        x = x + damping * (reduced_ref[at, :] - diag_ref[at, :] * x - coupled[p]) / scaling_ref[at, :]
        x_ref[at, :] = x
        new.append(x)
    if last:
        image_group(leaves, width, 0, m_refs[0][...], stack3(new), nodes, parent_ref, part_ref)
    else:
        image(leaves, width, km_ref, km3_ref, new, parent_ref, part_ref)


def add_kernel(x_ref, y_ref, tie_ref, out_ref):
    del tie_ref
    out_ref[...] = x_ref[...] + y_ref[...]


def leaf_kernel(leaves, y_ref, z_ref, rhs_ref, inverse_ref, *refs):
    out_ref = refs[-1]
    rest = rhs_ref[...] - (y_ref[...] + z_ref[...])
    for l in range(leaves):
        out_ref[pl.ds(l, 1), :] = rowdot(rest[l:l + 1, :], inverse_ref[l], True)


def join(blocks, tie):
    rows = blocks[0].shape[0]

    def kernel(*refs):
        out_ref = refs[-1]
        for n in range(len(blocks)):
            out_ref[pl.ds(n * rows, rows), :] = refs[n][...]

    return pl.pallas_call(
        kernel,
        out_shape=jax.ShapeDtypeStruct((len(blocks) * rows, blocks[0].shape[1]), blocks[0].dtype),
        in_specs=[VM] * (len(blocks) + 1),
        out_specs=VM,
        compiler_params=pltpu.CompilerParams(vmem_limit_bytes=16 * MIB),
        cost_estimate=NO_COST,
    )(*blocks, tie)


def in_vmem(x):
    return pltpu.with_memory_space_constraint(x, pltpu.VMEM)


def in_hbm(x):
    return pltpu.with_memory_space_constraint(x, pltpu.HBM)


def pick(info, places, source, ties):
    shape = jax.ShapeDtypeStruct(source.shape[1:], source.dtype)
    count = len(places)

    def kernel(place_ref, source_ref, *refs):
        first = len(ties)
        outs, token_ref = refs[first:first + count], refs[first + count]
        held, sem_in, sem_out = refs[first + count + 1:]
        token_ref[...] = jnp.zeros_like(token_ref)
        reads = [pltpu.make_async_copy(source_ref.at[place_ref[places[n]]], held.at[n], sem_in.at[n]) for n in range(count)]
        writes = [pltpu.make_async_copy(held.at[n], outs[n], sem_out.at[n]) for n in range(count)]
        for read in reads:
            read.start()
        for read, write in zip(reads, writes):
            read.wait()
            write.start()
        for write in writes:
            write.wait()

    return pl.pallas_call(
        kernel,
        out_shape=[shape] * count + [jax.ShapeDtypeStruct((8, 128), F32)],
        in_specs=[SM, HB] + [VM] * len(ties),
        out_specs=[HB] * count + [VM],
        scratch_shapes=[pltpu.VMEM((count,) + shape.shape, shape.dtype), pltpu.SemaphoreType.DMA((count,)),
                        pltpu.SemaphoreType.DMA((count,))],
        compiler_params=pltpu.CompilerParams(vmem_limit_bytes=12 * MIB),
        cost_estimate=NO_COST,
    )(info, in_hbm(source), *ties)


def leaf_spans(width, start, rows):
    spans = []
    while rows:
        size = min(rows, width - start % width)
        spans.append((start // width, start, size))
        start, rows = start + size, rows - size
    return spans


def product_kernel(leaves, width, terms, count, fresh, side, info_ref, parent_ref, *refs):
    m_refs, sources = refs[:4], refs[4:4 + count]
    outs, (u_ref, sem, out_sem) = refs[:-3][-2 - (side is not None):], refs[-3:]
    acc_ref, token_ref = outs[:2]
    work, late, slot = [], [], 0
    for k, n, entry, offset, start, rows in terms:
        if entry is None:
            ref, offset = sources[n], offset
        else:
            copy = pltpu.make_async_copy(sources[n].at[info_ref[entry]], u_ref.at[pl.ds(slot, rows)], sem.at[len(late)])
            copy.start()
            late.append(copy)
            ref, offset = u_ref, slot
            slot += rows
        spans = [(k, leaf, at, ref, offset + at - start, size) for leaf, at, size in leaf_spans(width, start, rows)]
        work = work + spans if entry is not None else spans + work
    token_ref[...] = jnp.zeros_like(token_ref)
    if fresh:
        acc_ref[...] = jnp.zeros_like(acc_ref)
    for k, leaf, at, ref, offset, size in work:
        if ref is u_ref:
            for copy in late:
                copy.wait()
            late = []
        value = lax.dot_general(m_refs[k][pl.ds(at, size), :], ref[pl.ds(offset, size), :], (((0,), (0,)), ((), ())),
                                preferred_element_type=F32)
        acc_ref[parent_ref[k * leaves + leaf]] += value
    if side is not None:
        nodes, rows, cols = acc_ref.shape
        where = info_ref[0] if side == 0 else 1 - info_ref[0]
        size = rows // 4
        pieces = [(p, pl.ds(i * size, size)) for p in range(nodes) for i in range(4)]
        for half in range(2):
            @pl.when(where == half)
            def _():
                for n, (p, at) in enumerate(pieces):
                    pltpu.make_async_copy(acc_ref.at[p, at], outs[2].at[p, at, pl.ds(half * cols, cols)], out_sem.at[n]).start()
        for n, (p, at) in enumerate(pieces):
            pltpu.make_async_copy(acc_ref.at[p, at], outs[2].at[p, at, pl.ds(0, cols)], out_sem.at[n]).wait()


def plane_body(scen, blk, link, leaf_inverse, leaf_rhs, node_rhs, node_diag, parent, tile_mask):
    leaves, width, cols = link.shape
    nodes = node_rhs.shape[0]
    base = leaves * width
    planes = blk // 2
    s, b = lax.axis_index("scen"), lax.axis_index("blk")
    z, core = b // 2, b % 2
    info = jnp.stack([core] + [2 * (s ^ k) + c for c in (core, 1 - core) for k in range(scen)]).astype(jnp.int32)

    def over_scen(x, k):
        return lax.ppermute(x, "scen", [(i, i ^ k) for i in range(scen)])

    def flip_z(x, k):
        return lax.ppermute(x, "blk", [(i, i ^ (2 * k)) for i in range(blk)])

    def flip_core(x):
        return lax.ppermute(x, "blk", [(i, i ^ 1) for i in range(blk)])

    masks = tile_mask.reshape(leaves)
    total = base + width + 4 * leaves
    cut = base // 2 + width // 8
    call = functools.partial(pl.pallas_call, cost_estimate=NO_COST, compiler_params=pltpu.CompilerParams(vmem_limit_bytes=16 * MIB))
    struct = jax.ShapeDtypeStruct
    bundle = call(
        functools.partial(start_kernel, leaves, width),
        out_shape=struct((total, cols), BF16),
        in_specs=[SM, SM, SM, VM, VM, VM],
        out_specs=VM,
        scratch_shapes=[pltpu.VMEM((4 * leaves, cols), F32)],
    )(info, in_hbm(masks), in_hbm(parent), in_hbm(link), in_hbm(leaf_inverse), in_hbm(leaf_rhs))
    parts = [5 * base // 8, 3 * base // 8]
    solved = call(
        functools.partial(solved_kernel, leaves, width),
        out_shape=[struct((rows, cols), BF16) for rows in parts],
        in_specs=[VM, VM],
        out_specs=[VM] * len(parts),
    )(in_hbm(leaf_inverse), bundle)
    gathered = [lax.all_gather(part, "blk") for part in solved]

    bx, by = over_scen(bundle, 1), over_scen(bundle, 2)
    da, db = over_scen(bx[:cut], 2), over_scen(by[cut:], 1)
    tops = [bx[base:], by[base:], db[base - cut:]]
    swap = flip_core(jnp.concatenate([t[:width] for t in tops[:2]], axis=0))
    swap3 = flip_core(tops[2][:width])
    notes = [t[width:, :width].astype(F32) for t in tops]
    owners = [parent] + [n[3 * leaves:, 0].astype(jnp.int32) for n in notes]
    parents = jnp.concatenate(owners)
    sides = [leaf_rhs] + [n[:leaves] + n[leaves:2 * leaves] + n[2 * leaves:3 * leaves] for n in notes]
    rights, rights3 = jnp.concatenate(sides[:3], axis=0), jnp.concatenate(sides, axis=0)

    count = scen * leaves
    node_shape, part_shape = pltpu.VMEM((nodes, cols), F32), pltpu.VMEM((count, width), F32)
    early_shape, late_shape = pltpu.VMEM((3 * base, cols), BF16), pltpu.VMEM((base, cols), BF16)
    terms_shape = pltpu.VMEM((3 * nodes, cols), F32)
    *m_all, km_all, diag, right = call(
        functools.partial(early_kernel, leaves, width, nodes),
        out_shape=[late_shape] * 3 + [early_shape, terms_shape, terms_shape],
        in_specs=[SM, SM] + [VM] * 6,
        out_specs=[VM] * 6,
        compiler_params=pltpu.CompilerParams(vmem_limit_bytes=16 * MIB),
    )(info, jnp.concatenate(owners[:3]), rights, leaf_inverse, bundle, bx, by, swap)
    def to_columns(gathered, ties):
        *blocks, token = pick(info, [1 + k for k in (1, 2, 3)], gathered, ties)
        return [over_scen(x, k + 1) for k, x in enumerate(blocks)], token

    m3, km3, reduced, scaling, current, part = call(
        functools.partial(late_kernel, leaves, width, cut),
        out_shape=[pltpu.HBM((base, cols), BF16)] * 2 + [node_shape, node_shape, node_shape, part_shape],
        in_specs=[SM, SM] + [VM] * 9,
        out_specs=[VM] * 6,
        compiler_params=pltpu.CompilerParams(vmem_limit_bytes=16 * MIB),
    )(info, parents, rights3, node_rhs, node_diag, da, db, swap3, in_vmem(km_all), diag, right)

    def exchange(x, tie=None):
        x = x + flip_core(x)
        other = flip_z(x, 1)
        x = x + other if tie is None else call(
            add_kernel, out_shape=pltpu.VMEM(x.shape, F32), in_specs=[VM] * 3, out_specs=VM)(x, other, tie)
        return x, flip_z(x, 2)

    def product(terms, sources, tie, acc=None, side=None, schur=None):
        held = [term for term in terms if term[2] is not None]
        dynamic = {term[1] for term in held}
        extra = [tie] + ([] if acc is None else [in_vmem(acc)]) + ([] if schur is None else [schur])
        first = 6 + len(sources)
        aliases = {} if acc is None else {first + 1: 0}
        if schur is not None:
            aliases[first + 2] = 2
        return call(
            functools.partial(product_kernel, leaves, width, terms, len(sources), acc is None, side),
            out_shape=[pltpu.VMEM((nodes, cols, cols), F32), pltpu.VMEM((8, 128), F32)]
            + ([] if side is None else [struct((nodes, cols, 2 * cols), F32)]),
            in_specs=[SM, SM] + [VM] * 4 + [HB if n in dynamic else VM for n in range(len(sources))]
            + [VM] * (1 + (acc is not None)) + [HB] * (schur is not None),
            out_specs=[VM, VM] + [HB] * (side is not None),
            scratch_shapes=[pltpu.VMEM((max(sum(term[-1] for term in held), 16), cols), BF16),
                            pltpu.SemaphoreType.DMA((max(len(held), 1),)), pltpu.SemaphoreType.DMA((4 * nodes,))],
            input_output_aliases=aliases,
            cost_estimate=pl.CostEstimate(flops=2 * sum(term[-1] for term in terms) * cols * cols, bytes_accessed=2 * MIB,
                                          transcendentals=0),
        )(info, parents, *map(in_vmem, (*m_all, m3)), *sources, *extra)

    def line_terms(side):
        return [(0, 0, 1 + side * scen, 0, 0, parts[0]), (0, 1, 1 + side * scen, 0, parts[0], parts[1])]

    own = [in_hbm(x) for x in gathered]
    first, token = to_columns(gathered[0], [part])
    arrived = exchange(part, token)
    ties = []
    for sweep in range(ITERS):
        last = sweep == ITERS - 1
        current, part = call(
            functools.partial(sweep_kernel, leaves, width, last, len(ties)),
            out_shape=[struct((nodes, cols), F32), pltpu.VMEM((leaves, width), F32)] if last else [node_shape, part_shape],
            in_specs=[SM] + [VM] * 12 + [VM if tie.dtype == F32 else HB for tie in ties],
            out_specs=[VM] * 2,
            compiler_params=pltpu.CompilerParams(vmem_limit_bytes=16 * MIB),
        )(parents, *arrived, reduced, scaling, node_diag, current, *map(in_vmem, (*m_all, m3, km_all, km3)), *ties)
        ties = []
        if sweep == 2:
            second, token = to_columns(gathered[1], [part])
            arrived = exchange(part, token)
            others = [flip_core(join(first, arrived[0]))]
            terms = line_terms(0) + [(k, 1 + k, None, 0, 0, parts[0]) for k in (1, 2, 3)]
            acc0, token = product(terms, own + first, arrived[0])
            ties = [token]
        elif last:
            terms = line_terms(1) + [(k, 2, None, (k - 1) * parts[0], 0, parts[0]) for k in (1, 2, 3)]
            acc1, token = product(terms, own + others, part)
            arrived = exchange(part, token)
            others = [flip_core(join(second, arrived[0]))]
            terms = [(k, k - 1, None, 0, parts[0], parts[1]) for k in (1, 2, 3)]
            unused, token, schur = product(terms, second, arrived[0], acc0, 0)
            ties = [token]
        else:
            arrived = exchange(part)
    leaf_solution = call(
        functools.partial(leaf_kernel, leaves),
        out_shape=struct((leaves, width), F32),
        in_specs=[VM] * 4 + [VM if tie.dtype == F32 else HB for tie in ties],
        out_specs=VM,
    )(*arrived, leaf_rhs, leaf_inverse, *ties)

    terms = [(k, 0, None, (k - 1) * parts[1], parts[0], parts[1]) for k in (1, 2, 3)]
    unused, token, schur = product(terms, others, arrived[0], acc1, 1, schur)
    return current, leaf_solution, schur


def solution(mesh):
    scen, blk = mesh.shape["scen"], mesh.shape["blk"]
    in_specs = (
        P("scen", None, "blk"),
        P("scen", None, None),
        P("scen", None),
        P(None, "blk"),
        P(None, "blk"),
        P("scen"),
        P("scen", "blk"),
    )
    out_specs = (P(None, "blk"), P("scen", None), P(None, "blk", "scen"))
    body = functools.partial(plane_body, scen, blk) if scen == 4 and blk == 2 * scen else general_body
    return jax.shard_map(body, mesh=mesh, in_specs=in_specs, out_specs=out_specs, check_vma=False)
```
